32 devices in a mesh: grp: 2 (over y), ep: 4 (over z), pp: 4 (over x, core).
Axes of the slice: x: 2, y: 2, z: 4, core: 2. Of those that a mesh axis runs over, the one named last changes fastest.
Arguments:
- hidden: bfloat16 [4, 256, 3584], P('pp', ('grp', 'ep')), parts along dimension 1, may hold values from -6 to 6
- norm_gain: bfloat16 [4, 3584], P('pp'), may hold values from 0.25 to 1.75
- expert_ids: int32 [4, 256, 2], P('pp', ('grp', 'ep')), parts along dimension 1, may hold values from 0 to 3, all different within a row; in each aligned block of 32 rows (0 to 31, 32 to 63, ..., all dimensions but the last counted through in order) at most 24 rows name the same one
- gate_weights: float32 [4, 256, 2], P('pp', ('grp', 'ep')), parts along dimension 1, may hold values from 0.1 to 0.6
- expert_gate_up: bfloat16 [4, 4, 3584, 2048], P('pp', 'ep'), may hold values from -0.09375 to 0.09375
- expert_down: bfloat16 [4, 4, 1024, 3584], P('pp', 'ep'), may hold values from -0.1875 to 0.1875
- partner: int32 [8, 16], P(('grp', 'ep')), parts along dimension 0, may hold values from 0 to 15, each once within a row
Outputs:
- passed: bfloat16 [4, 256, 3584], P('pp', ('grp', 'ep')), parts along dimension 1
The draws below stay inside these ranges and needn't reach their ends.
There are 2 independent parts, one for each index of `grp`. The reference program is written for one: setup_inputs(seed, part) draws one part's arguments, and reference() takes and returns one part's arrays. A program takes and returns all parts, laid end to end along the dimension named above; an argument that names none is the same for every part. Nothing has to cross between parts.
Inputs may be any that keep to these rules, and one draw needn't show every extreme that they name: `expert_ids`: each row names 2 different experts. Within the rows of one device (aligned blocks of 32 rows) no expert is named by more than 24 rows, and some block reaches 24. `partner`: the entries of each device's block are a permutation of the indices of its weak rows.
All inputs are finite; a program needn't handle non-finite values.
Results may differ from the reference program's by a relative error of at most 0.0034.
Values may be sent and summed in bfloat16 or wider, within the bound.
No kernel may reach another device: no remote copies, remote signals or barrier semaphores. Data moves between devices by JAX's collectives and lax.ppermute only.
A program may use at most 64 MiB of HBM per device.

```python
import math
import jax
import jax.numpy as jnp
import numpy as np
from jax import lax

D = 3584
HID = 1024
EXPERTS = 4
TOP = 2
ROWS_DEV = 32
LAYERS = 4
HSH = 1024
CAP = 24
ROWS = 128
N_EP = 4


def block_scale(stream_key, extent, split, low, largest):
    factor_of = 1.0
    for axis_at, blocks in split:
        heights = jax.random.uniform(jax.random.fold_in(jax.random.fold_in(stream_key, 6), axis_at), (blocks,), jnp.float32, low / len(split), largest / len(split))
        factor_of = factor_of * jnp.repeat(jnp.exp(heights), extent[axis_at] // blocks).reshape((-1,) + (1,) * (len(extent) - 1 - axis_at))
    return factor_of


def routed_block(stream_key, own, number, rows, number_of, top, most, slope):
    order = jax.random.permutation(stream_key, number_of)
    crowded, common = load_shares(number_of, rows * top, most, slope, True), load_shares(number_of, rows * top, most, slope, False)
    places = jnp.arange(number_of)

    def named(lengths, offset_by):
        used = int((lengths > 0).sum())
        fixed = max(1, used // 4)
        moved = fixed + (places - fixed + offset_by * (used - fixed)) % max(1, number_of - fixed)
        return jnp.zeros((number_of,), jnp.int32).at[order[jnp.where(places < fixed, places, moved)]].set(jnp.asarray(lengths, jnp.int32))

    lengths = jnp.where(number % 4 == 0, named(crowded, number // 4), named(common, number - number // 4 - 1))
    mixed = jax.random.permutation(jax.random.fold_in(own, 3), number_of)
    giver, sink = mixed[0:number_of // 2 * 2:2], mixed[1:number_of // 2 * 2:2]
    slack = jnp.minimum(lengths[giver] - 1, most - lengths[sink]) // 2
    slack = jnp.where((giver == order[0]) | (sink == order[0]) | (lengths[sink] == 0), 0, jnp.maximum(slack, 0))
    moved = jax.random.randint(jax.random.fold_in(own, 4), (number_of // 2,), 0, 1 << 20) % (slack + 1)
    lengths = lengths.at[giver].add(-moved).at[sink].add(moved)
    labels = jnp.searchsorted(jnp.cumsum(lengths), jnp.arange(rows * top), side="right").astype(jnp.int32)
    listing = labels.reshape(top, rows).T
    listing = listing[jax.random.permutation(jax.random.fold_in(own, 1), rows)]
    offset_by = jax.random.randint(jax.random.fold_in(own, 2), (rows, 1), 0, top)
    return jnp.take_along_axis(listing, (jnp.arange(top)[None, :] + offset_by) % top, axis=1)


def load_shares(amount, total, bound, lean, full):
    loads = [(1 << 20) // math.isqrt(grade ** lean) + 1 for grade in range(1, amount + 1)]
    largest = bound if full else min(bound, max(-(-total // amount), total * loads[0] // sum(loads)))
    least = 1 if total - largest >= amount - 1 else 0
    counts, spare = [largest] + [least] * (amount - 1), total - largest - least * (amount - 1)
    while spare > 0:
        candidates = [i for i in range(1, amount) if counts[i] < largest] or [i for i in range(1, amount) if counts[i] < bound]
        mass, left = sum([loads[i] for i in candidates]), spare
        for i in candidates:
            more = min(bound - counts[i], max(1, left * loads[i] // mass), spare)
            counts[i] = counts[i] + more
            spare = spare - more
    return np.array(counts)


def centred(rng, dims, deviation, reach, shards=(), kind=jnp.bfloat16):
    entries = jax.random.normal(rng, dims, jnp.float32) * deviation
    if len(shards) > 0:
        entries = block_scale(rng, dims, shards, -0.22, 0.18) * entries
    return jnp.clip(entries, min=-reach, max=reach).astype(kind)


def setup_inputs(seed: int = 0, part: int = 0) -> dict:
    splits = jax.random.split(jax.random.key(seed), 8)
    part_keys = jax.random.split(jax.random.fold_in(splits[7], part), 8)
    hidden = centred(part_keys[0], (LAYERS, ROWS, D), 1.0, 6.0, ((0, 4), (1, 4)))
    norm_gain = jnp.clip(1.0 + 0.15 * jax.random.normal(splits[1], (LAYERS, D), jnp.float32), 0.25, 1.75).astype(jnp.bfloat16)
    expert_ids_keys = jax.random.split(jax.random.fold_in(part_keys[2], 1), LAYERS * ROWS // ROWS_DEV)
    expert_ids_turns = jax.random.permutation(jax.random.fold_in(part_keys[2], 3), LAYERS * ROWS // ROWS_DEV)
    expert_ids = jax.vmap(lambda own, number: routed_block(jax.random.fold_in(part_keys[2], 2), own, number, ROWS_DEV, EXPERTS, TOP, CAP, 2))(expert_ids_keys, expert_ids_turns).reshape((LAYERS, ROWS, TOP))
    gate_weights = jnp.clip(0.1 + 0.5 * jax.random.uniform(part_keys[3], (LAYERS, ROWS, TOP), jnp.float32) ** block_scale(part_keys[3], (LAYERS, ROWS, TOP), ((0, 4), (1, 4)), -0.2, 0.2), 0.1, 0.6)
    expert_gate_up = centred(splits[4], (LAYERS, N_EP, D, 2 * HSH), D ** -0.5, 0.09375, ((0, 4), (1, 4)))
    expert_down = centred(splits[5], (LAYERS, N_EP, HSH, D), HID ** -0.5, 0.1875, ((0, 4), (1, 4)))
    partner = jax.vmap(lambda own: jax.random.permutation(own, ROWS_DEV // 2))(jax.random.split(part_keys[6], N_EP)).reshape((N_EP, ROWS_DEV // 2)).astype(jnp.int32)
    return {"hidden": hidden, "norm_gain": norm_gain, "expert_ids": expert_ids, "gate_weights": gate_weights, "expert_gate_up": expert_gate_up, "expert_down": expert_down, "partner": partner}


guidance_scale = 2.5
epsilon = 1e-06

def normalize(section_rows, section_gain):
    widened = section_rows.astype(jnp.float32)
    factor = lax.rsqrt(lax.optimization_barrier(jnp.mean(widened * widened, axis=-1, keepdims=True)) + epsilon)
    return (widened * factor * section_gain.astype(jnp.float32)).astype(jnp.bfloat16)

def section_layer(section_rows, section_gain, section_ids, section_gates, section_gate_up, section_down):
    widened = section_rows.astype(jnp.float32)
    normed = normalize(section_rows, section_gain)
    shard_width = section_down.shape[1]
    row_total = section_rows.shape[0]
    slot_bound = N_EP * CAP
    shards_each = N_EP // EXPERTS

    def one_slice(mixture, slice_index):
        expert = slice_index // shards_each
        naming = section_ids == expert
        weight = lax.optimization_barrier(jnp.sum(jnp.where(naming, section_gates, 0.0), axis=1))
        present = jnp.any(naming, axis=1)
        named_count = jnp.sum(present.astype(jnp.int32))
        chosen_rows = jnp.nonzero(present, size=slot_bound, fill_value=0)[0].astype(jnp.int32)
        filled_slot = jnp.arange(slot_bound, dtype=jnp.int32) < named_count
        picked_weight = jnp.where(filled_slot, jnp.take(weight, chosen_rows), 0.0)
        inputs = jnp.take(normed, chosen_rows, axis=0)
        gate_up = lax.dynamic_index_in_dim(section_gate_up, slice_index, 0, keepdims=False)
        down_matrix = lax.dynamic_index_in_dim(section_down, slice_index, 0, keepdims=False)
        projected = jnp.dot(inputs, gate_up, preferred_element_type=jnp.float32)
        active = (jax.nn.silu(projected[:, :shard_width]) * projected[:, shard_width:]).astype(jnp.bfloat16)
        output = jnp.dot(active, down_matrix, preferred_element_type=jnp.float32).astype(jnp.bfloat16)
        mixture = mixture.at[chosen_rows].add(picked_weight[:, None] * output.astype(jnp.float32))
        return (mixture, None)
    mixture, _ = lax.scan(one_slice, jnp.zeros((row_total, D), jnp.float32), jnp.arange(N_EP, dtype=jnp.int32))
    return widened + mixture

def reference(hidden, norm_gain, expert_ids, gate_weights, expert_gate_up, expert_down, partner):
    results = []
    for section_index in range(LAYERS):
        layer_out = section_layer(hidden[section_index], norm_gain[section_index], expert_ids[section_index], gate_weights[section_index], expert_gate_up[section_index], expert_down[section_index])
        if section_index == LAYERS - 1:
            blocks = layer_out.reshape(N_EP, ROWS_DEV, D)
            middle = ROWS_DEV // 2
            weak_rows = blocks[:, middle:]
            paired = jax.vmap(lambda source, ordering: jnp.take(source, ordering, axis=0))(weak_rows, partner.astype(jnp.int32))
            guided = paired + guidance_scale * (blocks[:, :middle] - paired)
            layer_out = jnp.concatenate([guided, weak_rows], axis=1).reshape(ROWS, D)
        results.append(layer_out.astype(jnp.bfloat16))
    return jnp.roll(jnp.stack(results), 1, axis=0)
```

```python
import functools

import jax
import jax.numpy as jnp
from jax import lax
from jax.experimental import pallas as pl
from jax.experimental.pallas import tpu as pltpu
from jax.sharding import PartitionSpec as P

EXPERTS = 4
TOP = 2
CAP = 24

guidance_scale = 2.5
epsilon = 1e-06
F32 = jnp.float32
BF16 = jnp.bfloat16
VMEM = pl.BlockSpec(memory_space=pltpu.VMEM)
SMEM = pl.BlockSpec(memory_space=pltpu.SMEM)


def chunk_of(extent, largest):
    size = largest
    while extent % size:
        size //= 2
    return size


def offset_target(me, offset, devices):
    if devices & (devices - 1) == 0:
        return me ^ offset
    return (me + offset) % devices


def route_kernel(devices, place, hidden, gain, ids, gates, partner, *outs):
    picked, mix = outs[:-1], outs[-1]
    rows, width = hidden.shape
    middle = rows // 2
    widened = hidden[...].astype(F32)
    factor = lax.rsqrt(jnp.mean(widened * widened, axis=-1, keepdims=True) + epsilon)
    normed = (widened * factor * gain[...].astype(F32)).astype(BF16)

    shards_each = devices // EXPERTS
    me, is_last = place[0], place[1]
    line = lax.broadcasted_iota(jnp.int32, (rows, rows), 0)
    lane = lax.broadcasted_iota(jnp.int32, (rows, rows), 1)
    before = (line < lane).astype(F32)
    expert = lax.broadcasted_iota(jnp.int32, (EXPERTS, rows), 0)
    named = jnp.zeros((EXPERTS, rows), F32)
    weight = jnp.zeros((EXPERTS, rows), F32)
    for k in range(TOP):
        same = ids[k : k + 1, :] == expert
        named = named + same.astype(F32)
        weight = weight + jnp.where(same, gates[k : k + 1, :], 0.0)
    position = jnp.dot(named, before, preferred_element_type=F32)
    position = jnp.where(named > 0.0, position, -1.0)

    slot = lax.broadcasted_iota(jnp.int32, (CAP, rows), 0).astype(F32)
    choices, weighted = [], [(line == lane).astype(F32)]
    for offset in range(devices):
        own = offset_target(me, offset, devices) // shards_each
        mine = expert == own
        where_to = jnp.sum(jnp.where(mine, position, 0.0), axis=0, keepdims=True)
        share = jnp.sum(jnp.where(mine, weight, 0.0), axis=0, keepdims=True)
        choice = (where_to == slot).astype(F32)
        choices.append(choice)
        weighted.append(choice * share)
    for offset in range(devices):
        picked[offset][...] = jnp.dot(
            choices[offset].astype(BF16), normed, preferred_element_type=F32
        ).astype(BF16)

    pair_line = lax.broadcasted_iota(jnp.int32, (rows, middle), 0)
    pair_lane = lax.broadcasted_iota(jnp.int32, (rows, middle), 1)
    pair = jnp.sum(
        jnp.where(pair_line == pair_lane, partner[...].astype(F32), 0.0), axis=1, keepdims=True
    )
    same_row = (line == lane).astype(F32)
    weak_row = (lane.astype(F32) == pair + float(middle)).astype(F32)
    guided = guidance_scale * same_row + (1.0 - guidance_scale) * weak_row
    guide = jnp.where(jnp.logical_and(line < middle, is_last > 0), guided, same_row)
    mix[...] = lax.dot_general(
        guide,
        jnp.concatenate(weighted, axis=0),
        (((1,), (1,)), ((), ())),
        precision=lax.Precision.HIGHEST,
        preferred_element_type=F32,
    )


def route(place, hidden, gain, ids, gates, partner, devices):
    rows, width = hidden.shape
    return pl.pallas_call(
        functools.partial(route_kernel, devices),
        out_shape=[jax.ShapeDtypeStruct((CAP, width), BF16)] * devices
        + [jax.ShapeDtypeStruct((rows, rows + devices * CAP), F32)],
        in_specs=[SMEM] + [VMEM] * 5,
        out_specs=[VMEM] * (devices + 1),
        compiler_params=pltpu.CompilerParams(vmem_limit_bytes=16 << 20),
    )(place, hidden, gain, ids, gates, partner)


def expert_kernel(count, step, *refs):
    rows = refs[:count]
    gate_up, down = refs[count : count + 2]
    outs = refs[count + 2 :]
    half = down.shape[0]
    stacked = jnp.concatenate([r[...].astype(F32) for r in rows], axis=0).astype(BF16)
    projected = jnp.dot(stacked, gate_up[...], preferred_element_type=F32)
    gate, up = projected[:, :half], projected[:, half:]
    active = (gate / (1.0 + jnp.exp(-gate)) * up).astype(BF16)

    def columns(i, carry):
        at = pl.ds(pl.multiple_of(i * step, step), step)
        part = jnp.dot(active, down[:, at], preferred_element_type=F32)
        for k in range(count):
            outs[k][:, at] = part[k * CAP : (k + 1) * CAP].astype(BF16)
        return carry

    lax.fori_loop(0, down.shape[1] // step, columns, 0)


def experts(rows, gate_up, down):
    count = len(rows)
    width = down.shape[1]
    total = count * CAP
    return pl.pallas_call(
        functools.partial(expert_kernel, count, chunk_of(width, 512)),
        out_shape=[jax.ShapeDtypeStruct((CAP, width), BF16)] * count,
        in_specs=[VMEM] * (count + 2),
        out_specs=[VMEM] * count,
        compiler_params=pltpu.CompilerParams(vmem_limit_bytes=(8 << 20) + total * width * 8),
        cost_estimate=pl.CostEstimate(
            flops=2 * total * (gate_up.size + down.size),
            bytes_accessed=2 * (gate_up.size + down.size),
            transcendentals=total * down.shape[0],
        ),
    )(*rows, gate_up, down)


def combine_kernel(count, step, mix, hidden, *refs):
    slots, out = refs[:count], refs[count]
    high = mix[...].astype(BF16)
    low = (mix[...] - high.astype(F32)).astype(BF16)

    def columns(i, carry):
        at = pl.ds(pl.multiple_of(i * step, step), step)
        stacked = jnp.concatenate(
            [hidden[:, at].astype(F32)] + [s[:, at].astype(F32) for s in slots], axis=0
        ).astype(BF16)
        out[:, at] = (
            jnp.dot(high, stacked, preferred_element_type=F32)
            + jnp.dot(low, stacked, preferred_element_type=F32)
        ).astype(BF16)
        return carry

    lax.fori_loop(0, out.shape[1] // step, columns, 0)


def combine(mix, hidden, slots):
    count = len(slots)
    rows, width = hidden.shape
    return pl.pallas_call(
        functools.partial(combine_kernel, count, chunk_of(width, 512)),
        out_shape=jax.ShapeDtypeStruct((rows, width), BF16),
        in_specs=[VMEM] * (count + 2),
        out_specs=VMEM,
        compiler_params=pltpu.CompilerParams(vmem_limit_bytes=16 << 20),
    )(mix, hidden, *slots)


def shards(hidden, norm_gain, expert_ids, gate_weights, expert_gate_up, expert_down, partner):
    devices = lax.axis_size("ep")
    sections = lax.axis_size("pp")
    place = jnp.stack(
        [lax.axis_index("ep"), (lax.axis_index("pp") == sections - 1).astype(jnp.int32)]
    )
    section_rows = hidden[0]
    gate_up = expert_gate_up[0, 0]
    down = expert_down[0, 0]

    *picked, mix = route(
        place, section_rows, norm_gain, expert_ids[0].T, gate_weights[0].T, partner, devices
    )

    def onward(value):
        return lax.ppermute(value, "pp", [(i, (i + 1) % sections) for i in range(sections)])

    def dispatch(value, offset):
        if offset == 0:
            return value
        return lax.ppermute(
            value, "ep", [(i, offset_target(i, offset, devices)) for i in range(devices)]
        )

    def send_back(value, offset):
        return lax.ppermute(
            value,
            ("ep", "pp"),
            [
                (offset_target(i, offset, devices) * sections + p, i * sections + (p + 1) % sections)
                for i in range(devices)
                for p in range(sections)
            ],
        )

    split = max(1, devices * 3 // 4)
    order = [devices // 2] + [k for k in range(split, devices)]
    order += [k for k in range(devices) if k not in order]
    arrived = {}
    for k in order:
        arrived[k] = dispatch(picked[k], k)
    hidden_before = onward(section_rows)
    mix_before = onward(mix)

    returned = {}
    for group in (range(0, split), range(split, devices)):
        if len(group):
            results = experts([arrived[k] for k in group], gate_up, down)
            for k in sorted(group, key=lambda j: order.index(j)):
                returned[k] = send_back(results[k - group[0]], k)
    out = combine(mix_before, hidden_before, [returned[k] for k in range(devices)])
    return out[None]


def solution(mesh):
    return jax.shard_map(
        shards,
        mesh=mesh,
        in_specs=(
            P("pp", ("grp", "ep"), None),
            P("pp", None),
            P("pp", ("grp", "ep"), None),
            P("pp", ("grp", "ep"), None),
            P("pp", "ep", None, None),
            P("pp", "ep", None, None),
            P(("grp", "ep"), None),
        ),
        out_specs=P("pp", ("grp", "ep"), None),
        check_vma=False,
    )
```

```python
import functools

import jax
import jax.numpy as jnp
from jax import lax
from jax.experimental import pallas as pl
from jax.experimental.pallas import tpu as pltpu
from jax.sharding import PartitionSpec as P

EXPERTS = 4
TOP = 2
CAP = 24

guidance_scale = 2.5
epsilon = 1e-06
F32 = jnp.float32
BF16 = jnp.bfloat16
VMEM = pl.BlockSpec(memory_space=pltpu.VMEM)
SMEM = pl.BlockSpec(memory_space=pltpu.SMEM)
HBM = pl.BlockSpec(memory_space=pltpu.HBM)


def chunk_of(extent, largest):
    size = largest
    while extent % size:
        size //= 2
    return size


def in_hbm(*arrays):
    return [pltpu.with_memory_space_constraint(a, pltpu.HBM) for a in arrays]


def lanes_for(extent):
    return -(-extent // 128) * 128


def offset_target(me, offset, devices):
    if devices & (devices - 1) == 0:
        return me ^ offset
    return (me + offset) % devices


def fetch(pairs, sems):
    copies = [pltpu.make_async_copy(s, d, sems.at[i]) for i, (s, d) in enumerate(pairs)]
    for copy in copies:
        copy.start()
    for copy in copies:
        copy.wait()


def slot_positions(ids, rows):
    line = lax.broadcasted_iota(jnp.int32, (rows, rows), 0)
    lane = lax.broadcasted_iota(jnp.int32, (rows, rows), 1)
    expert = lax.broadcasted_iota(jnp.int32, (EXPERTS, rows), 0)
    named = jnp.zeros((EXPERTS, rows), F32)
    for k in range(TOP):
        named = named + (ids[k : k + 1, :] == expert).astype(F32)
    position = jnp.dot(named, (line < lane).astype(F32), preferred_element_type=F32)
    return jnp.where(named > 0.0, position, -1.0)


def of_expert(table, own):
    expert = lax.broadcasted_iota(jnp.int32, table.shape, 0)
    return jnp.sum(jnp.where(expert == own, table, 0.0), axis=0, keepdims=True)


def choice_of(position, own, rows):
    slot = lax.broadcasted_iota(jnp.int32, (CAP, rows), 0).astype(F32)
    return (of_expert(position, own) == slot).astype(F32)


def pick(choice, normed):
    return jnp.dot(choice.astype(BF16), normed, preferred_element_type=F32).astype(BF16)


def first_kernel(devices, offset, place, hidden_at, gain_at, ids_at, picked, normed, hidden, gain, ids, sems):
    fetch([(ids_at, ids), (gain_at, gain), (hidden_at, hidden)], sems)
    rows, _ = hidden.shape
    own = offset_target(place[0], offset, devices) // (devices // EXPERTS)
    choice = choice_of(slot_positions(ids, rows), own, rows)
    widened = hidden[...].astype(F32)
    factor = lax.rsqrt(jnp.mean(widened * widened, axis=-1, keepdims=True) + epsilon)
    normed[...] = (widened * factor * gain[...].astype(F32)).astype(BF16)
    picked[...] = pick(choice, normed[...])


def route_first(place, hidden, gain, ids, devices, offset):
    rows, width = hidden.shape
    return pl.pallas_call(
        functools.partial(first_kernel, devices, offset),
        out_shape=[
            jax.ShapeDtypeStruct((CAP, width), BF16),
            jax.ShapeDtypeStruct((rows, width), BF16),
        ],
        in_specs=[SMEM] + [HBM] * 3,
        out_specs=[VMEM] * 2,
        scratch_shapes=[
            pltpu.VMEM(hidden.shape, BF16),
            pltpu.VMEM(gain.shape, BF16),
            pltpu.VMEM(ids.shape, jnp.int32),
            pltpu.SemaphoreType.DMA((3,)),
        ],
        compiler_params=pltpu.CompilerParams(vmem_limit_bytes=8 << 20),
    )(place, *in_hbm(hidden, gain, ids))


def rest_kernel(devices, offsets, place, normed, hidden_at, ids_at, gates_at, partner_at, *refs):
    picked, packed = refs[: len(offsets)], refs[len(offsets)]
    ids, gates, partner, sems = refs[len(offsets) + 1 :]
    rows, width = normed.shape
    fetch(
        [
            (ids_at, ids),
            (gates_at, gates),
            (partner_at, partner),
            (hidden_at, packed.at[:, pl.ds(0, width)]),
        ],
        sems,
    )
    middle = rows // 2
    me, is_last = place[0], place[1]
    position = slot_positions(ids, rows)
    expert = lax.broadcasted_iota(jnp.int32, (EXPERTS, rows), 0)
    weight = jnp.zeros((EXPERTS, rows), F32)
    for k in range(TOP):
        weight = weight + jnp.where(ids[k : k + 1, :] == expert, gates[k : k + 1, :], 0.0)

    line = lax.broadcasted_iota(jnp.int32, (rows, rows), 0)
    lane = lax.broadcasted_iota(jnp.int32, (rows, rows), 1)
    same_row = (line == lane).astype(F32)
    weighted = [same_row]
    for offset in range(devices):
        own = offset_target(me, offset, devices) // (devices // EXPERTS)
        choice = choice_of(position, own, rows)
        weighted.append(choice * of_expert(weight, own))
        if offset in offsets:
            picked[offsets.index(offset)][...] = pick(choice, normed[...])

    pair_line = lax.broadcasted_iota(jnp.int32, (rows, middle), 0)
    pair_lane = lax.broadcasted_iota(jnp.int32, (rows, middle), 1)
    pair = jnp.sum(
        jnp.where(pair_line == pair_lane, partner[...].astype(F32), 0.0), axis=1, keepdims=True
    )
    weak_row = (lane.astype(F32) == pair + float(middle)).astype(F32)
    guided = guidance_scale * same_row + (1.0 - guidance_scale) * weak_row
    guide = jnp.where(jnp.logical_and(line < middle, is_last > 0), guided, same_row)
    span = (packed.shape[1] - width) // 2
    if span > rows + devices * CAP:
        weighted.append(jnp.zeros((span - rows - devices * CAP, rows), F32))
    mix = lax.dot_general(
        guide,
        jnp.concatenate(weighted, axis=0),
        (((1,), (1,)), ((), ())),
        precision=lax.Precision.HIGHEST,
        preferred_element_type=F32,
    )
    high = mix.astype(BF16)
    packed[:, width : width + span] = high
    packed[:, width + span :] = (mix - high.astype(F32)).astype(BF16)


def route_rest(place, normed, hidden, ids, gates, partner, devices, offsets):
    rows, width = normed.shape
    span = lanes_for(rows + devices * CAP)
    return pl.pallas_call(
        functools.partial(rest_kernel, devices, offsets),
        out_shape=[jax.ShapeDtypeStruct((CAP, width), BF16)] * len(offsets)
        + [jax.ShapeDtypeStruct((rows, width + 2 * span), BF16)],
        in_specs=[SMEM, VMEM] + [HBM] * 4,
        out_specs=[VMEM] * (len(offsets) + 1),
        scratch_shapes=[
            pltpu.VMEM(ids.shape, jnp.int32),
            pltpu.VMEM(gates.shape, F32),
            pltpu.VMEM(partner.shape, jnp.int32),
            pltpu.SemaphoreType.DMA((4,)),
        ],
        compiler_params=pltpu.CompilerParams(vmem_limit_bytes=8 << 20),
    )(place, normed, *in_hbm(hidden, ids, gates, partner))


def load_kernel(parts, source, held, sems):
    size = source.shape[0] // parts
    fetch(
        [(source.at[pl.ds(i * size, size)], held.at[pl.ds(i * size, size)]) for i in range(parts)],
        sems,
    )


def load(matrix):
    parts = 7 if matrix.shape[0] % 112 == 0 else 1
    return pl.pallas_call(
        functools.partial(load_kernel, parts),
        out_shape=pltpu.VMEM(matrix.shape, matrix.dtype),
        in_specs=[HBM],
        out_specs=VMEM,
        scratch_shapes=[pltpu.SemaphoreType.DMA((parts,))],
        compiler_params=pltpu.CompilerParams(vmem_limit_bytes=1 << 20),
        cost_estimate=pl.CostEstimate(
            flops=0, bytes_accessed=2 * matrix.size, transcendentals=0
        ),
    )(*in_hbm(matrix))


def expert_kernel(count, step, loads, *refs):
    rows = refs[:count]
    gate_up, down = refs[count : count + 2]
    outs = refs[count + 2 : 2 * count + 2]
    if loads:
        held, sem = refs[2 * count + 2 :]
        copy = pltpu.make_async_copy(down, held, sem)
        copy.start()
    half = down.shape[0]
    stacked = jnp.concatenate([r[...].astype(F32) for r in rows], axis=0).astype(BF16)
    projected = jnp.dot(stacked, gate_up[...], preferred_element_type=F32)
    gate, up = projected[:, :half], projected[:, half:]
    active = (gate / (1.0 + jnp.exp(-gate)) * up).astype(BF16)
    if loads:
        copy.wait()
    else:
        held = down

    def columns(i, carry):
        at = pl.ds(pl.multiple_of(i * step, step), step)
        part = jnp.dot(active, held[:, at], preferred_element_type=F32)
        for k in range(count):
            outs[k][:, at] = part[k * CAP : (k + 1) * CAP].astype(BF16)
        return carry

    lax.fori_loop(0, down.shape[1] // step, columns, 0)


def experts(rows, gate_up, down, loads):
    count = len(rows)
    width = down.shape[1]
    total = count * CAP
    return pl.pallas_call(
        functools.partial(expert_kernel, count, chunk_of(width, 512), loads),
        out_shape=[jax.ShapeDtypeStruct((CAP, width), BF16)] * count
        + [pltpu.VMEM(down.shape, down.dtype)] * loads,
        in_specs=[VMEM] * (count + 1) + [HBM if loads else VMEM],
        out_specs=[VMEM] * (count + loads),
        scratch_shapes=[pltpu.SemaphoreType.DMA] * loads,
        compiler_params=pltpu.CompilerParams(vmem_limit_bytes=(6 << 20) + total * width * 8),
        cost_estimate=pl.CostEstimate(
            flops=2 * total * (gate_up.size + down.size),
            bytes_accessed=2 * (gate_up.size + down.size),
            transcendentals=total * down.shape[0],
        ),
    )(*rows, gate_up, *(in_hbm(down) if loads else [down]))


def combine_kernel(count, step, packed, *refs):
    slots, out = refs[:count], refs[count]
    rows, width = out.shape
    span = (packed.shape[1] - width) // 2
    used = rows + count * CAP
    high = packed[:, width : width + span][:, :used]
    low = packed[:, width + span :][:, :used]

    def columns(i, carry):
        at = pl.ds(pl.multiple_of(i * step, step), step)
        stacked = jnp.concatenate(
            [packed[:, at].astype(F32)] + [s[:, at].astype(F32) for s in slots], axis=0
        ).astype(BF16)
        out[:, at] = (
            jnp.dot(high, stacked, preferred_element_type=F32)
            + jnp.dot(low, stacked, preferred_element_type=F32)
        ).astype(BF16)
        return carry

    lax.fori_loop(0, width // step, columns, 0)


def combine(packed, slots):
    count = len(slots)
    rows, width = packed.shape[0], slots[0].shape[1]
    return pl.pallas_call(
        functools.partial(combine_kernel, count, chunk_of(width, 512)),
        out_shape=jax.ShapeDtypeStruct((rows, width), BF16),
        in_specs=[VMEM] * (count + 1),
        out_specs=VMEM,
        compiler_params=pltpu.CompilerParams(vmem_limit_bytes=8 << 20),
    )(packed, *slots)


def shards(hidden, norm_gain, expert_ids, gate_weights, expert_gate_up, expert_down, partner):
    devices = lax.axis_size("ep")
    sections = lax.axis_size("pp")
    place = jnp.stack(
        [lax.axis_index("ep"), (lax.axis_index("pp") == sections - 1).astype(jnp.int32)]
    )
    section_rows = hidden[0]
    gate_up = expert_gate_up[0, 0]
    down = expert_down[0, 0]

    far = devices // 2
    others = [k for k in range(devices - 1, -1, -1) if k != far]
    ids, gates = expert_ids[0].T, gate_weights[0].T
    picked = {}
    picked[far], normed = route_first(place, section_rows, norm_gain, ids, devices, far)
    *rest, packed = route_rest(
        place, normed, section_rows, ids, gates, partner, devices, others
    )
    picked.update(zip(others, rest))

    def onward(value):
        return lax.ppermute(value, "pp", [(i, (i + 1) % sections) for i in range(sections)])

    def dispatch(value, offset):
        if offset == 0:
            return value
        return lax.ppermute(
            value, "ep", [(i, offset_target(i, offset, devices)) for i in range(devices)]
        )

    def send_back(value, offset):
        return lax.ppermute(
            value,
            ("ep", "pp"),
            [
                (offset_target(i, offset, devices) * sections + p, i * sections + (p + 1) % sections)
                for i in range(devices)
                for p in range(sections)
            ],
        )

    arrived = {k: dispatch(picked[k], k) for k in [far] + others}
    gate_up = load(gate_up)
    packed, gate_up = lax.optimization_barrier((packed, gate_up))
    packed = onward(packed)

    split = max(1, devices * 3 // 4)
    early = [k for k in range(split) if k != far]
    late = list(range(split, devices))
    returned = {}
    *results, down = experts([arrived[k] for k in [far] + early], gate_up, down, True)
    for k, result in zip([far] + early, results):
        returned[k] = send_back(result, k)
    results = experts([arrived[k] for k in late], gate_up, down, False)
    for k, result in zip(late, results):
        returned[k] = send_back(result, k)
    out = combine(packed, [returned[k] for k in range(devices)])
    return out[None]


def solution(mesh):
    return jax.shard_map(
        shards,
        mesh=mesh,
        in_specs=(
            P("pp", ("grp", "ep"), None),
            P("pp", None),
            P("pp", ("grp", "ep"), None),
            P("pp", ("grp", "ep"), None),
            P("pp", "ep", None, None),
            P("pp", "ep", None, None),
            P(("grp", "ep"), None),
        ),
        out_specs=P("pp", ("grp", "ep"), None),
        check_vma=False,
    )
```

```python
import functools

import jax
import jax.numpy as jnp
from jax import lax
from jax.experimental import pallas as pl
from jax.experimental.pallas import tpu as pltpu
from jax.sharding import PartitionSpec as P

EXPERTS = 4
TOP = 2
CAP = 24
OWN = 32
AHEAD = 8

guidance_scale = 2.5
epsilon = 1e-06
F32 = jnp.float32
BF16 = jnp.bfloat16
VMEM = pl.BlockSpec(memory_space=pltpu.VMEM)
SMEM = pl.BlockSpec(memory_space=pltpu.SMEM)
HBM = pl.BlockSpec(memory_space=pltpu.HBM)


def chunk_of(extent, largest):
    size = largest
    while extent % size:
        size //= 2
    return size


def in_hbm(*arrays):
    return [pltpu.with_memory_space_constraint(a, pltpu.HBM) for a in arrays]


def lanes_for(extent):
    return -(-extent // 128) * 128


def offset_target(me, offset, devices):
    if devices & (devices - 1) == 0:
        return me ^ offset
    return (me + offset) % devices


def fetch(pairs, sems, others=()):
    copies = [pltpu.make_async_copy(s, d, sems.at[i]) for i, (s, d) in enumerate(pairs)]
    for copy in [*copies, *others]:
        copy.start()
    for copy in copies:
        copy.wait()


def slot_positions(ids, rows):
    line = lax.broadcasted_iota(jnp.int32, (rows, rows), 0)
    lane = lax.broadcasted_iota(jnp.int32, (rows, rows), 1)
    expert = lax.broadcasted_iota(jnp.int32, (EXPERTS, rows), 0)
    named = jnp.zeros((EXPERTS, rows), F32)
    for k in range(TOP):
        named = named + (ids[k : k + 1, :] == expert).astype(F32)
    position = jnp.dot(named, (line < lane).astype(F32), preferred_element_type=F32)
    return jnp.where(named > 0.0, position, -1.0)


def of_expert(table, own):
    expert = lax.broadcasted_iota(jnp.int32, table.shape, 0)
    return jnp.sum(jnp.where(expert == own, table, 0.0), axis=0, keepdims=True)


def choice_of(position, own, rows):
    slot = lax.broadcasted_iota(jnp.int32, (CAP, rows), 0).astype(F32)
    return (of_expert(position, own) == slot).astype(F32)


def pick(choice, normed):
    return jnp.dot(choice.astype(BF16), normed, preferred_element_type=F32).astype(BF16)


def first_kernel(devices, offsets, place, hidden_at, gain_at, ids_at, *refs):
    picked, (normed, hidden, gain, ids, sems) = refs[: len(offsets)], refs[len(offsets) :]
    pairs = [(ids_at, ids), (hidden_at, hidden), (gain_at, gain)]
    copies = [pltpu.make_async_copy(s, d, sems.at[i]) for i, (s, d) in enumerate(pairs)]
    for copy in copies:
        copy.start()
    rows, _ = hidden.shape
    copies[0].wait()
    position = slot_positions(ids, rows)
    owners = [offset_target(place[0], k, devices) // (devices // EXPERTS) for k in offsets]
    choices = [choice_of(position, own, rows) for own in owners]
    copies[1].wait()
    copies[2].wait()
    widened = hidden[...].astype(F32)
    factor = lax.rsqrt(jnp.mean(widened * widened, axis=-1, keepdims=True) + epsilon)
    normed[...] = (widened * factor * gain[...].astype(F32)).astype(BF16)
    for ref, choice in zip(picked, choices):
        ref[...] = pick(choice, normed[...])


def route_first(place, hidden, gain, ids, devices, offsets):
    rows, width = hidden.shape
    return pl.pallas_call(
        functools.partial(first_kernel, devices, offsets),
        out_shape=[jax.ShapeDtypeStruct((CAP, width), BF16)] * len(offsets)
        + [jax.ShapeDtypeStruct((rows, width), BF16)],
        in_specs=[SMEM] + [HBM] * 3,
        out_specs=[VMEM] * (len(offsets) + 1),
        scratch_shapes=[
            pltpu.VMEM(hidden.shape, BF16),
            pltpu.VMEM(gain.shape, BF16),
            pltpu.VMEM(ids.shape, jnp.int32),
            pltpu.SemaphoreType.DMA((3,)),
        ],
        compiler_params=pltpu.CompilerParams(vmem_limit_bytes=8 << 20),
    )(place, *in_hbm(hidden, gain, ids))


def rest_kernel(
    devices, offsets, parts, place, normed, hidden_at, ids_at, gates_at, partner_at, weights_at, *refs
):
    picked, (packed, weights) = refs[: len(offsets)], refs[len(offsets) : len(offsets) + 2]
    ids, gates, partner, sems, weight_sems = refs[len(offsets) + 2 :]
    rows, width = normed.shape
    size = weights.shape[0] // parts
    copies = [
        pltpu.make_async_copy(
            weights_at.at[pl.ds(i * size, size)], weights.at[pl.ds(i * size, size)], weight_sems.at[i]
        )
        for i in range(parts)
    ]
    fetch(
        [
            (ids_at, ids),
            (gates_at, gates),
            (partner_at, partner),
            (hidden_at, packed.at[pl.ds(0, rows), pl.ds(0, width)]),
        ],
        sems,
        copies,
    )
    middle = rows // 2
    me, is_last = place[0], place[1]
    position = slot_positions(ids, rows)
    expert = lax.broadcasted_iota(jnp.int32, (EXPERTS, rows), 0)
    weight = jnp.zeros((EXPERTS, rows), F32)
    for k in range(TOP):
        weight = weight + jnp.where(ids[k : k + 1, :] == expert, gates[k : k + 1, :], 0.0)

    line = lax.broadcasted_iota(jnp.int32, (rows, rows), 0)
    lane = lax.broadcasted_iota(jnp.int32, (rows, rows), 1)
    same_row = (line == lane).astype(F32)
    weighted = [same_row]
    for offset in range(devices):
        own = offset_target(me, offset, devices) // (devices // EXPERTS)
        choice = choice_of(position, own, rows)
        weighted.append(choice * of_expert(weight, own))
        if offset in offsets:
            picked[offsets.index(offset)][...] = pick(choice, normed[...])

    pair_line = lax.broadcasted_iota(jnp.int32, (rows, middle), 0)
    pair_lane = lax.broadcasted_iota(jnp.int32, (rows, middle), 1)
    pair = jnp.sum(
        jnp.where(pair_line == pair_lane, partner[...].astype(F32), 0.0), axis=1, keepdims=True
    )
    weak_row = (lane.astype(F32) == pair + float(middle)).astype(F32)
    guided = guidance_scale * same_row + (1.0 - guidance_scale) * weak_row
    guide = jnp.where(jnp.logical_and(line < middle, is_last > 0), guided, same_row)
    span = (packed.shape[1] - width) // 2
    if span > rows + devices * CAP:
        weighted.append(jnp.zeros((span - rows - devices * CAP, rows), F32))
    mix = lax.dot_general(
        guide,
        jnp.concatenate(weighted, axis=0),
        (((1,), (1,)), ((), ())),
        precision=lax.Precision.HIGHEST,
        preferred_element_type=F32,
    )
    high = mix.astype(BF16)
    packed[:rows, width : width + span] = high
    packed[:rows, width + span :] = (mix - high.astype(F32)).astype(BF16)
    packed[rows:, :] = jnp.zeros((OWN, packed.shape[1]), BF16)
    for copy in copies:
        copy.wait()


def route_rest(place, normed, hidden, ids, gates, partner, weights, devices, offsets):
    parts = 7 if weights.shape[0] % 112 == 0 else 1
    rows, width = normed.shape
    span = lanes_for(rows + devices * CAP)
    return pl.pallas_call(
        functools.partial(rest_kernel, devices, offsets, parts),
        out_shape=[jax.ShapeDtypeStruct((CAP, width), BF16)] * len(offsets)
        + [jax.ShapeDtypeStruct((rows + OWN, width + 2 * span), BF16)]
        + [pltpu.VMEM(weights.shape, weights.dtype)],
        in_specs=[SMEM, VMEM] + [HBM] * 5,
        out_specs=[VMEM] * (len(offsets) + 2),
        scratch_shapes=[
            pltpu.VMEM(ids.shape, jnp.int32),
            pltpu.VMEM(gates.shape, F32),
            pltpu.VMEM(partner.shape, jnp.int32),
            pltpu.SemaphoreType.DMA((4,)),
            pltpu.SemaphoreType.DMA((parts,)),
        ],
        compiler_params=pltpu.CompilerParams(vmem_limit_bytes=8 << 20),
        cost_estimate=pl.CostEstimate(
            flops=0, bytes_accessed=2 * weights.size, transcendentals=0
        ),
    )(place, normed, *in_hbm(hidden, ids, gates, partner, weights))


def hidden_units(rows, weights):
    stacked = jnp.concatenate([r[...].astype(F32) for r in rows], axis=0).astype(BF16)
    projected = jnp.dot(stacked, weights[...], preferred_element_type=F32)
    half = projected.shape[1] // 2
    gate, up = projected[:, :half], projected[:, half:]
    return (gate / (1.0 + jnp.exp(-gate)) * up).astype(BF16)


def early_kernel(count, step, *refs):
    rows, (packed_in, gate_up, down_at) = refs[:count], refs[count : count + 3]
    outs, (packed, down, down_sem) = refs[count + 3 : 2 * count + 2], refs[2 * count + 2 :]
    copy = pltpu.make_async_copy(down_at, down, down_sem)
    copy.start()
    active = hidden_units(rows, gate_up)
    own_at = packed.shape[0] - OWN
    copy.wait()
    for i in range(down.shape[1] // step):
        at = pl.ds(i * step, step)
        part = jnp.dot(active, down[:, at], preferred_element_type=F32)
        for k in range(count - 1):
            outs[k][:, at] = part[k * CAP : (k + 1) * CAP].astype(BF16)
        own = jnp.concatenate([part[(count - 1) * CAP :], jnp.zeros((OWN - CAP, step), F32)], axis=0)
        packed[own_at:, at] = own.astype(BF16)


def early_experts(rows, packed, gate_up, down):
    count = len(rows)
    width = down.shape[1]
    total = count * CAP
    *results, packed, down = pl.pallas_call(
        functools.partial(early_kernel, count, chunk_of(width, 512)),
        out_shape=[jax.ShapeDtypeStruct((CAP, width), BF16)] * (count - 1)
        + [jax.ShapeDtypeStruct(packed.shape, BF16), pltpu.VMEM(down.shape, down.dtype)],
        in_specs=[VMEM] * (count + 2) + [HBM],
        out_specs=[VMEM] * (count + 1),
        input_output_aliases={count: count - 1},
        scratch_shapes=[pltpu.SemaphoreType.DMA],
        compiler_params=pltpu.CompilerParams(vmem_limit_bytes=(6 << 20) + total * width * 8),
        cost_estimate=pl.CostEstimate(
            flops=2 * total * (gate_up.size + down.size),
            bytes_accessed=2 * (gate_up.size + down.size),
            transcendentals=total * down.shape[0],
        ),
    )(*rows, packed, gate_up, *in_hbm(down))
    return results, packed, down


def late_kernel(count, step, *refs):
    rows, (gate_up, down), outs = refs[:count], refs[count : count + 2], refs[count + 2 :]
    active = hidden_units(rows, gate_up)
    for i in range(down.shape[1] // step):
        at = pl.ds(i * step, step)
        part = jnp.dot(active, down[:, at], preferred_element_type=F32)
        for k in range(count):
            outs[k][:, at] = part[k * CAP : (k + 1) * CAP].astype(BF16)


def late_experts(rows, gate_up, down):
    count = len(rows)
    width = down.shape[1]
    total = count * CAP
    return pl.pallas_call(
        functools.partial(late_kernel, count, chunk_of(width, 512)),
        out_shape=[jax.ShapeDtypeStruct((CAP, width), BF16)] * count,
        in_specs=[VMEM] * (count + 2),
        out_specs=[VMEM] * count,
        compiler_params=pltpu.CompilerParams(vmem_limit_bytes=(6 << 20) + total * width * 8),
        cost_estimate=pl.CostEstimate(
            flops=2 * AHEAD * total * (gate_up.size + down.size),
            bytes_accessed=2 * AHEAD * (gate_up.size + down.size),
            transcendentals=total * down.shape[0],
        ),
    )(*rows, gate_up, down)


def combine_kernel(count, step, packed, *refs):
    slots, out_at, out, sems = refs[:count], *refs[count:]
    rows, width = out.shape
    span = (packed.shape[1] - width) // 2
    used = rows + (count + 1) * CAP
    high = packed[:rows, width : width + span][:, :used]
    low = packed[:rows, width + span :][:, :used]

    def copy(i):
        at = pl.ds(i * step, step)
        return pltpu.make_async_copy(out.at[:, at], out_at.at[:, at], sems.at[i])

    for i in range(width // step):
        at = pl.ds(i * step, step)
        stacked = jnp.concatenate(
            [packed[:rows, at].astype(F32), packed[rows:, at].astype(F32)[:CAP]]
            + [s[:, at].astype(F32) for s in slots],
            axis=0,
        ).astype(BF16)
        out[:, at] = (
            jnp.dot(high, stacked, preferred_element_type=F32)
            + jnp.dot(low, stacked, preferred_element_type=F32)
        ).astype(BF16)
        copy(i).start()
    for i in range(width // step):
        copy(i).wait()


def combine(packed, slots):
    count = len(slots)
    rows, width = packed.shape[0] - OWN, slots[0].shape[1]
    step = chunk_of(width, 512)
    return pl.pallas_call(
        functools.partial(combine_kernel, count, step),
        out_shape=jax.ShapeDtypeStruct((rows, width), BF16),
        in_specs=[VMEM] * (count + 1),
        out_specs=HBM,
        scratch_shapes=[
            pltpu.VMEM((rows, width), BF16),
            pltpu.SemaphoreType.DMA((width // step,)),
        ],
        compiler_params=pltpu.CompilerParams(vmem_limit_bytes=8 << 20),
    )(packed, *slots)


def shards(hidden, norm_gain, expert_ids, gate_weights, expert_gate_up, expert_down, partner):
    devices = lax.axis_size("ep")
    sections = lax.axis_size("pp")
    place = jnp.stack(
        [lax.axis_index("ep"), (lax.axis_index("pp") == sections - 1).astype(jnp.int32)]
    )
    section_rows = hidden[0]
    gate_up = expert_gate_up[0, 0]
    down = expert_down[0, 0]

    far, split = devices // 2, max(1, devices * 3 // 4)
    early = [far] + [k for k in range(1, split) if k != far]
    late = list(range(split, devices))
    ids, gates = expert_ids[0].T, gate_weights[0].T
    *picked, normed = route_first(place, section_rows, norm_gain, ids, devices, early)
    *rest, packed, gate_up = route_rest(
        place, normed, section_rows, ids, gates, partner, gate_up, devices, late + [0]
    )
    picked = dict(zip(early + late + [0], picked + rest))

    def onward(value):
        return lax.ppermute(value, "pp", [(i, (i + 1) % sections) for i in range(sections)])

    def dispatch(value, offset):
        if offset == 0:
            return value
        return lax.ppermute(
            value, "ep", [(i, offset_target(i, offset, devices)) for i in range(devices)]
        )

    def send_back(value, offset):
        return lax.ppermute(
            value,
            ("ep", "pp"),
            [
                (offset_target(i, offset, devices) * sections + p, i * sections + (p + 1) % sections)
                for i in range(devices)
                for p in range(sections)
            ],
        )

    arrived = {k: dispatch(picked[k], k) for k in early + late + [0]}
    results, packed, down = early_experts(
        [arrived[k] for k in early + [0]], packed, gate_up, down
    )
    returned = {k: send_back(result, k) for k, result in zip(early, results)}
    packed = onward(packed)
    results = late_experts([arrived[k] for k in late], gate_up, down)
    returned.update({k: send_back(result, k) for k, result in zip(late, results)})
    out = combine(packed, [returned[k] for k in range(1, devices)])
    return out[None]


def solution(mesh):
    return jax.shard_map(
        shards,
        mesh=mesh,
        in_specs=(
            P("pp", ("grp", "ep"), None),
            P("pp", None),
            P("pp", ("grp", "ep"), None),
            P("pp", ("grp", "ep"), None),
            P("pp", "ep", None, None),
            P("pp", "ep", None, None),
            P(("grp", "ep"), None),
        ),
        out_specs=P("pp", ("grp", "ep"), None),
        check_vma=False,
    )
```

```python
import functools

import jax
import jax.numpy as jnp
from jax import lax
from jax.experimental import pallas as pl
from jax.experimental.pallas import tpu as pltpu
from jax.sharding import PartitionSpec as P

EXPERTS = 4
TOP = 2
CAP = 24
AHEAD = 8

guidance_scale = 2.5
epsilon = 1e-06
F32 = jnp.float32
BF16 = jnp.bfloat16
VMEM = pl.BlockSpec(memory_space=pltpu.VMEM)
HBM = pl.BlockSpec(memory_space=pltpu.HBM)


def chunk_of(extent, largest):
    size = largest
    while extent % size:
        size //= 2
    return size


def in_hbm(*arrays):
    return [pltpu.with_memory_space_constraint(a, pltpu.HBM) for a in arrays]


def lanes_for(extent):
    return -(-extent // 128) * 128


def offset_target(me, offset, devices):
    if devices & (devices - 1) == 0:
        return me ^ offset
    return (me + offset) % devices


def fetch(pairs, sems, others=()):
    copies = [pltpu.make_async_copy(s, d, sems.at[i]) for i, (s, d) in enumerate(pairs)]
    for copy in [*copies, *others]:
        copy.start()
    for copy in copies:
        copy.wait()


def slot_positions(ids, rows):
    line = lax.broadcasted_iota(jnp.int32, (rows, rows), 0)
    lane = lax.broadcasted_iota(jnp.int32, (rows, rows), 1)
    expert = lax.broadcasted_iota(jnp.int32, (EXPERTS, rows), 0)
    named = jnp.zeros((EXPERTS, rows), F32)
    for k in range(TOP):
        named = named + (ids[k : k + 1, :] == expert).astype(F32)
    position = jnp.dot(
        named.astype(BF16), (line < lane).astype(F32).astype(BF16), preferred_element_type=F32
    )
    return jnp.where(named > 0.0, position, -1.0)


def of_expert(table, own):
    expert = lax.broadcasted_iota(jnp.int32, table.shape, 0)
    return jnp.sum(jnp.where(expert == own, table, 0.0), axis=0, keepdims=True)


def choice_of(position, own, rows):
    slot = lax.broadcasted_iota(jnp.int32, (CAP, rows), 0).astype(F32)
    return (of_expert(position, own) == slot).astype(F32)


def pick(choice, rows):
    return jnp.dot(choice.astype(BF16), rows, preferred_element_type=F32).astype(BF16)


def first_kernel(devices, offsets, hidden_at, ids_at, *refs):
    picked, (hidden, ids, sems) = refs[: len(offsets)], refs[len(offsets) :]
    pairs = [(ids_at, ids), (hidden_at, hidden)]
    copies = [pltpu.make_async_copy(s, d, sems.at[i]) for i, (s, d) in enumerate(pairs)]
    for copy in copies:
        copy.start()
    rows, _ = hidden.shape
    copies[0].wait()
    position = slot_positions(ids, rows)
    me = lax.axis_index("ep")
    owners = [offset_target(me, k, devices) // (devices // EXPERTS) for k in offsets]
    choices = jnp.concatenate([choice_of(position, own, rows) for own in owners], axis=0)
    copies[1].wait()
    taken = jnp.dot(choices.astype(BF16), hidden[...], preferred_element_type=F32)
    for k, ref in enumerate(picked):
        ref[...] = taken[k * CAP : (k + 1) * CAP].astype(BF16)


def route_first(hidden, ids, devices, offsets):
    rows, width = hidden.shape
    return pl.pallas_call(
        functools.partial(first_kernel, devices, offsets),
        out_shape=[jax.ShapeDtypeStruct((CAP, width), BF16)] * len(offsets)
        + [pltpu.VMEM((rows, width), BF16)],
        in_specs=[HBM] * 2,
        out_specs=[VMEM] * (len(offsets) + 1),
        scratch_shapes=[pltpu.VMEM(ids.shape, jnp.int32), pltpu.SemaphoreType.DMA((2,))],
        compiler_params=pltpu.CompilerParams(vmem_limit_bytes=8 << 20),
    )(*in_hbm(hidden, ids))


def rest_kernel(
    devices, offsets, order, parts, hidden, ids_at, gates_at, partner_at, gain_at, weights_at, *refs
):
    picked, (packed, gain, weights) = refs[: len(offsets)], refs[len(offsets) : len(offsets) + 3]
    ids, gates, partner, sems, weight_sems = refs[len(offsets) + 3 :]
    rows, width = hidden.shape
    size = weights.shape[0] // parts
    copies = [
        pltpu.make_async_copy(
            weights_at.at[pl.ds(i * size, size)], weights.at[pl.ds(i * size, size)], weight_sems.at[i]
        )
        for i in range(parts)
    ]
    fetch(
        [
            (ids_at, ids),
            (gates_at, gates),
            (partner_at, partner),
            (gain_at, gain),
        ],
        sems,
        copies,
    )
    middle = rows // 2
    me = lax.axis_index("ep")
    is_last = (lax.axis_index("pp") == lax.axis_size("pp") - 1).astype(jnp.int32)
    position = slot_positions(ids, rows)
    expert = lax.broadcasted_iota(jnp.int32, (EXPERTS, rows), 0)
    weight = jnp.zeros((EXPERTS, rows), F32)
    for k in range(TOP):
        weight = weight + jnp.where(ids[k : k + 1, :] == expert, gates[k : k + 1, :], 0.0)

    line = lax.broadcasted_iota(jnp.int32, (rows, rows), 0)
    lane = lax.broadcasted_iota(jnp.int32, (rows, rows), 1)
    same_row = (line == lane).astype(F32)
    weighted = [same_row]
    for offset in order:
        own = offset_target(me, offset, devices) // (devices // EXPERTS)
        choice = choice_of(position, own, rows)
        weighted.append(choice * of_expert(weight, own))
        if offset in offsets:
            picked[offsets.index(offset)][...] = pick(choice, hidden[...])

    pair_line = lax.broadcasted_iota(jnp.int32, (rows, middle), 0)
    pair_lane = lax.broadcasted_iota(jnp.int32, (rows, middle), 1)
    pair = jnp.sum(
        jnp.where(pair_line == pair_lane, partner[...].astype(F32), 0.0), axis=1, keepdims=True
    )
    weak_row = (lane.astype(F32) == pair + float(middle)).astype(F32)
    guided = guidance_scale * same_row + (1.0 - guidance_scale) * weak_row
    guide = jnp.where(jnp.logical_and(line < middle, is_last > 0), guided, same_row)
    span = (packed.shape[1] - width) // 2
    if span > rows + devices * CAP:
        weighted.append(jnp.zeros((span - rows - devices * CAP, rows), F32))
    mix = lax.dot_general(
        guide,
        jnp.concatenate(weighted, axis=0),
        (((1,), (1,)), ((), ())),
        precision=lax.Precision.HIGHEST,
        preferred_element_type=F32,
    )
    high = mix.astype(BF16)
    packed[:, :width] = hidden[...]
    packed[:, width : width + span] = high
    packed[:, width + span :] = (mix - high.astype(F32)).astype(BF16)
    for copy in copies:
        copy.wait()


def route_rest(hidden, ids, gates, partner, gain, weights, devices, offsets, order):
    parts = 7 if weights.shape[0] % 112 == 0 else 1
    rows, width = hidden.shape
    span = lanes_for(rows + devices * CAP)
    return pl.pallas_call(
        functools.partial(rest_kernel, devices, offsets, order, parts),
        out_shape=[jax.ShapeDtypeStruct((CAP, width), BF16)] * len(offsets)
        + [jax.ShapeDtypeStruct((rows, width + 2 * span), BF16)]
        + [pltpu.VMEM(gain.shape, gain.dtype), pltpu.VMEM(weights.shape, weights.dtype)],
        in_specs=[VMEM] + [HBM] * 5,
        out_specs=[VMEM] * (len(offsets) + 3),
        scratch_shapes=[
            pltpu.VMEM(ids.shape, jnp.int32),
            pltpu.VMEM(gates.shape, F32),
            pltpu.VMEM(partner.shape, jnp.int32),
            pltpu.SemaphoreType.DMA((4,)),
            pltpu.SemaphoreType.DMA((parts,)),
        ],
        compiler_params=pltpu.CompilerParams(vmem_limit_bytes=8 << 20),
        cost_estimate=pl.CostEstimate(
            flops=0, bytes_accessed=2 * weights.size, transcendentals=0
        ),
    )(hidden, *in_hbm(ids, gates, partner, gain, weights))


def hidden_units(rows, gain, weights):
    stacked = jnp.concatenate([r[...].astype(F32) for r in rows], axis=0)
    factor = lax.rsqrt(jnp.mean(stacked * stacked, axis=-1, keepdims=True) + epsilon)
    normed = (stacked * factor * gain[...].astype(F32)).astype(BF16)
    projected = jnp.dot(normed, weights[...], preferred_element_type=F32)
    half = projected.shape[1] // 2
    gate, up = projected[:, :half], projected[:, half:]
    return (gate / (1.0 + jnp.exp(-gate)) * up).astype(BF16)


def early_kernel(count, step, *refs):
    rows, (gain, gate_up, down_at) = refs[:count], refs[count : count + 3]
    outs, (down, down_sem) = refs[count + 3 : 2 * count + 3], refs[2 * count + 3 :]
    copy = pltpu.make_async_copy(down_at, down, down_sem)
    copy.start()
    active = hidden_units(rows, gain, gate_up)
    copy.wait()
    for i in range(down.shape[1] // step):
        at = pl.ds(i * step, step)
        part = jnp.dot(active, down[:, at], preferred_element_type=F32)
        for k in range(count):
            outs[k][:, at] = part[k * CAP : (k + 1) * CAP].astype(BF16)


def early_experts(rows, gain, gate_up, down):
    count = len(rows)
    width = down.shape[1]
    total = count * CAP
    *results, down = pl.pallas_call(
        functools.partial(early_kernel, count, chunk_of(width, 512)),
        out_shape=[jax.ShapeDtypeStruct((CAP, width), BF16)] * count
        + [pltpu.VMEM(down.shape, down.dtype)],
        in_specs=[VMEM] * (count + 2) + [HBM],
        out_specs=[VMEM] * (count + 1),
        scratch_shapes=[pltpu.SemaphoreType.DMA],
        compiler_params=pltpu.CompilerParams(vmem_limit_bytes=(6 << 20) + total * width * 8),
        cost_estimate=pl.CostEstimate(
            flops=2 * total * (gate_up.size + down.size),
            bytes_accessed=2 * (gate_up.size + down.size),
            transcendentals=total * down.shape[0],
        ),
    )(*rows, gain, gate_up, *in_hbm(down))
    return results, down


def late_kernel(count, step, *refs):
    rows, (gain, gate_up, down), outs = refs[:count], refs[count : count + 3], refs[count + 3 :]
    active = hidden_units(rows, gain, gate_up)
    for i in range(down.shape[1] // step):
        at = pl.ds(i * step, step)
        part = jnp.dot(active, down[:, at], preferred_element_type=F32)
        for k in range(count):
            outs[k][:, at] = part[k * CAP : (k + 1) * CAP].astype(BF16)


def late_experts(rows, gain, gate_up, down):
    count = len(rows)
    width = down.shape[1]
    total = count * CAP
    return pl.pallas_call(
        functools.partial(late_kernel, count, chunk_of(width, 512)),
        out_shape=[jax.ShapeDtypeStruct((CAP, width), BF16)] * count,
        in_specs=[VMEM] * (count + 3),
        out_specs=[VMEM] * count,
        compiler_params=pltpu.CompilerParams(vmem_limit_bytes=(6 << 20) + total * width * 8),
        cost_estimate=pl.CostEstimate(
            flops=2 * AHEAD * total * (gate_up.size + down.size),
            bytes_accessed=2 * AHEAD * (gate_up.size + down.size),
            transcendentals=total * down.shape[0],
        ),
    )(*rows, gain, gate_up, down)


def mixing(packed, width, at, used):
    span = (packed.shape[1] - width) // 2
    high = packed[:, width : width + span].astype(F32)[:, at : at + used]
    low = packed[:, width + span :].astype(F32)[:, at : at + used]
    return jnp.concatenate([high, low], axis=0).astype(BF16)


def mixed(matrix, stacked):
    both = jnp.dot(matrix, stacked.astype(BF16), preferred_element_type=F32)
    rows = both.shape[0] // 2
    return both[:rows] + both[rows:]


def begin_kernel(count, step, packed, *refs):
    slots, total = refs[:count], refs[count]
    rows, width = total.shape
    matrix = mixing(packed, width, 0, rows + count * CAP)
    for i in range(width // step):
        at = pl.ds(i * step, step)
        stacked = jnp.concatenate(
            [packed[:, at].astype(F32)] + [s[:, at].astype(F32) for s in slots], axis=0
        )
        total[:, at] = mixed(matrix, stacked)


def begin_combine(packed, slots):
    count = len(slots)
    rows, width = packed.shape[0], slots[0].shape[1]
    return pl.pallas_call(
        functools.partial(begin_kernel, count, chunk_of(width, 512)),
        out_shape=jax.ShapeDtypeStruct((rows, width), F32),
        in_specs=[VMEM] * (count + 1),
        out_specs=VMEM,
        compiler_params=pltpu.CompilerParams(vmem_limit_bytes=8 << 20),
    )(packed, *slots)


def finish_kernel(count, step, begin, packed, total, *refs):
    slots, out_at, out, sems = refs[:count], *refs[count:]
    rows, width = out.shape
    matrix = mixing(packed, width, begin, count * CAP)

    def copy(i):
        at = pl.ds(i * step, step)
        return pltpu.make_async_copy(out.at[:, at], out_at.at[:, at], sems.at[i])

    for i in range(width // step):
        at = pl.ds(i * step, step)
        stacked = jnp.concatenate([s[:, at].astype(F32) for s in slots], axis=0)
        out[:, at] = (total[:, at] + mixed(matrix, stacked)).astype(BF16)
        copy(i).start()
    for i in range(width // step):
        copy(i).wait()


def finish_combine(packed, total, slots, begin):
    count = len(slots)
    rows, width = total.shape
    step = chunk_of(width, 512)
    return pl.pallas_call(
        functools.partial(finish_kernel, count, step, begin),
        out_shape=jax.ShapeDtypeStruct((rows, width), BF16),
        in_specs=[VMEM] * (count + 2),
        out_specs=HBM,
        scratch_shapes=[
            pltpu.VMEM((rows, width), BF16),
            pltpu.SemaphoreType.DMA((width // step,)),
        ],
        compiler_params=pltpu.CompilerParams(vmem_limit_bytes=8 << 20),
    )(packed, total, *slots)


def shards(hidden, norm_gain, expert_ids, gate_weights, expert_gate_up, expert_down, partner):
    devices = lax.axis_size("ep")
    sections = lax.axis_size("pp")
    section_rows = hidden[0]
    gate_up = expert_gate_up[0, 0]
    down = expert_down[0, 0]

    far, split = devices // 2, max(1, devices * 3 // 4)
    early = [far] + [k for k in range(1, split) if k != far]
    late = list(range(split, devices))
    ids, gates = expert_ids[0].T, gate_weights[0].T
    *picked, rows = route_first(section_rows, ids, devices, early)
    *rest, packed, gain, gate_up = route_rest(
        rows,
        ids,
        gates,
        partner,
        norm_gain,
        gate_up,
        devices,
        late + [0],
        early[::-1] + late + [0],
    )
    picked = dict(zip(early + late + [0], picked + rest))

    def onward(value):
        return lax.ppermute(value, "pp", [(i, (i + 1) % sections) for i in range(sections)])

    def dispatch(value, offset):
        if offset == 0:
            return value
        return lax.ppermute(
            value, "ep", [(i, offset_target(i, offset, devices)) for i in range(devices)]
        )

    def send_back(value, offset):
        return lax.ppermute(
            value,
            ("ep", "pp"),
            [
                (offset_target(i, offset, devices) * sections + p, i * sections + (p + 1) % sections)
                for i in range(devices)
                for p in range(sections)
            ],
        )

    arrived = {k: dispatch(picked[k], k) for k in early + late + [0]}
    packed = onward(packed)
    results, down = early_experts([arrived[k] for k in early + [0]], gain, gate_up, down)
    results = dict(zip(early + [0], results))
    returned = {k: send_back(results[k], k) for k in early[::-1]}
    packed, *held = lax.optimization_barrier((packed, *[arrived[k] for k in late]))
    results.update(zip(late, late_experts(held, gain, gate_up, down)))
    last = late + [0]
    for k, result in zip(last, lax.optimization_barrier([results[k] for k in last])):
        returned[k] = send_back(result, k)
    total = begin_combine(packed, [returned[k] for k in early[::-1]])
    begin = section_rows.shape[0] + len(early) * CAP
    out = finish_combine(packed, total, [returned[k] for k in late + [0]], begin)
    return out[None]


def solution(mesh):
    return jax.shard_map(
        shards,
        mesh=mesh,
        in_specs=(
            P("pp", ("grp", "ep"), None),
            P("pp", None),
            P("pp", ("grp", "ep"), None),
            P("pp", ("grp", "ep"), None),
            P("pp", "ep", None, None),
            P("pp", "ep", None, None),
            P(("grp", "ep"), None),
        ),
        out_specs=P("pp", ("grp", "ep"), None),
        check_vma=False,
    )
```

```python
import functools

import jax
import jax.numpy as jnp
from jax import lax
from jax.experimental import pallas as pl
from jax.experimental.pallas import tpu as pltpu
from jax.sharding import PartitionSpec as P

EXPERTS = 4
TOP = 2
CAP = 24
AHEAD = 8

guidance_scale = 2.5
epsilon = 1e-06
F32 = jnp.float32
BF16 = jnp.bfloat16
VMEM = pl.BlockSpec(memory_space=pltpu.VMEM)
HBM = pl.BlockSpec(memory_space=pltpu.HBM)


def chunk_of(extent, largest):
    size = largest
    while extent % size:
        size //= 2
    return size


def in_hbm(*arrays):
    return [pltpu.with_memory_space_constraint(a, pltpu.HBM) for a in arrays]


def lanes_for(extent):
    return -(-extent // 128) * 128


def offset_target(me, offset, devices):
    if devices & (devices - 1) == 0:
        return me ^ offset
    return (me + offset) % devices


def fetch(pairs, sems, others=()):
    copies = [pltpu.make_async_copy(s, d, sems.at[i]) for i, (s, d) in enumerate(pairs)]
    for copy in [*copies, *others]:
        copy.start()
    for copy in copies:
        copy.wait()


def slot_positions(ids, rows):
    line = lax.broadcasted_iota(jnp.int32, (rows, rows), 0)
    lane = lax.broadcasted_iota(jnp.int32, (rows, rows), 1)
    expert = lax.broadcasted_iota(jnp.int32, (EXPERTS, rows), 0)
    named = jnp.zeros((EXPERTS, rows), F32)
    for k in range(TOP):
        named = named + (ids[k : k + 1, :] == expert).astype(F32)
    position = jnp.dot(
        named.astype(BF16), (line < lane).astype(F32).astype(BF16), preferred_element_type=F32
    )
    return jnp.where(named > 0.0, position, -1.0)


def of_expert(table, own):
    expert = lax.broadcasted_iota(jnp.int32, table.shape, 0)
    return jnp.sum(jnp.where(expert == own, table, 0.0), axis=0, keepdims=True)


def choice_of(position, own, rows):
    slot = lax.broadcasted_iota(jnp.int32, (CAP, rows), 0).astype(F32)
    return (of_expert(position, own) == slot).astype(F32)


def pick(choice, rows):
    return jnp.dot(choice.astype(BF16), rows, preferred_element_type=F32).astype(BF16)


def first_kernel(devices, offsets, hidden_at, ids_at, *refs):
    picked, (hidden, ids, sems) = refs[: len(offsets)], refs[len(offsets) :]
    pairs = [(ids_at, ids), (hidden_at, hidden)]
    copies = [pltpu.make_async_copy(s, d, sems.at[i]) for i, (s, d) in enumerate(pairs)]
    for copy in copies:
        copy.start()
    rows, _ = hidden.shape
    copies[0].wait()
    position = slot_positions(ids, rows)
    me = lax.axis_index("ep")
    owners = [offset_target(me, k, devices) // (devices // EXPERTS) for k in offsets]
    choices = jnp.concatenate([choice_of(position, own, rows) for own in owners], axis=0)
    copies[1].wait()
    taken = jnp.dot(choices.astype(BF16), hidden[...], preferred_element_type=F32)
    for k, ref in enumerate(picked):
        ref[...] = taken[k * CAP : (k + 1) * CAP].astype(BF16)


def route_first(hidden, ids, devices, offsets):
    rows, width = hidden.shape
    return pl.pallas_call(
        functools.partial(first_kernel, devices, offsets),
        out_shape=[jax.ShapeDtypeStruct((CAP, width), BF16)] * len(offsets)
        + [pltpu.VMEM((rows, width), BF16)],
        in_specs=[HBM] * 2,
        out_specs=[VMEM] * (len(offsets) + 1),
        scratch_shapes=[pltpu.VMEM(ids.shape, jnp.int32), pltpu.SemaphoreType.DMA((2,))],
        compiler_params=pltpu.CompilerParams(vmem_limit_bytes=8 << 20),
    )(*in_hbm(hidden, ids))


def rest_kernel(
    devices, offsets, order, parts, hidden, ids_at, gates_at, partner_at, gain_at, weights_at, *refs
):
    picked, (packed, gain, weights) = refs[: len(offsets)], refs[len(offsets) : len(offsets) + 3]
    ids, gates, partner, sems, weight_sems = refs[len(offsets) + 3 :]
    rows, width = hidden.shape
    size = weights.shape[0] // parts
    copies = [
        pltpu.make_async_copy(
            weights_at.at[pl.ds(i * size, size)], weights.at[pl.ds(i * size, size)], weight_sems.at[i]
        )
        for i in range(parts)
    ]
    fetch(
        [
            (ids_at, ids),
            (gates_at, gates),
            (partner_at, partner),
            (gain_at, gain),
        ],
        sems,
        copies,
    )
    middle = rows // 2
    me = lax.axis_index("ep")
    is_last = (lax.axis_index("pp") == lax.axis_size("pp") - 1).astype(jnp.int32)
    position = slot_positions(ids, rows)
    expert = lax.broadcasted_iota(jnp.int32, (EXPERTS, rows), 0)
    weight = jnp.zeros((EXPERTS, rows), F32)
    for k in range(TOP):
        weight = weight + jnp.where(ids[k : k + 1, :] == expert, gates[k : k + 1, :], 0.0)

    line = lax.broadcasted_iota(jnp.int32, (rows, rows), 0)
    lane = lax.broadcasted_iota(jnp.int32, (rows, rows), 1)
    same_row = (line == lane).astype(F32)
    weighted = [same_row]
    for offset in order:
        own = offset_target(me, offset, devices) // (devices // EXPERTS)
        choice = choice_of(position, own, rows)
        weighted.append(choice * of_expert(weight, own))
        if offset in offsets:
            picked[offsets.index(offset)][...] = pick(choice, hidden[...])

    pair_line = lax.broadcasted_iota(jnp.int32, (rows, middle), 0)
    pair_lane = lax.broadcasted_iota(jnp.int32, (rows, middle), 1)
    pair = jnp.sum(
        jnp.where(pair_line == pair_lane, partner[...].astype(F32), 0.0), axis=1, keepdims=True
    )
    weak_row = (lane.astype(F32) == pair + float(middle)).astype(F32)
    guided = guidance_scale * same_row + (1.0 - guidance_scale) * weak_row
    guide = jnp.where(jnp.logical_and(line < middle, is_last > 0), guided, same_row)
    span = (packed.shape[1] - width) // 2
    if span > rows + devices * CAP:
        weighted.append(jnp.zeros((span - rows - devices * CAP, rows), F32))
    mix = lax.dot_general(
        guide,
        jnp.concatenate(weighted, axis=0),
        (((1,), (1,)), ((), ())),
        precision=lax.Precision.HIGHEST,
        preferred_element_type=F32,
    )
    high = mix.astype(BF16)
    packed[:, :width] = hidden[...]
    packed[:, width : width + span] = high
    packed[:, width + span :] = (mix - high.astype(F32)).astype(BF16)
    for copy in copies:
        copy.wait()


def route_rest(hidden, ids, gates, partner, gain, weights, devices, offsets, order):
    parts = 7 if weights.shape[0] % 112 == 0 else 1
    rows, width = hidden.shape
    span = lanes_for(rows + devices * CAP)
    return pl.pallas_call(
        functools.partial(rest_kernel, devices, offsets, order, parts),
        out_shape=[jax.ShapeDtypeStruct((CAP, width), BF16)] * len(offsets)
        + [jax.ShapeDtypeStruct((rows, width + 2 * span), BF16)]
        + [pltpu.VMEM(gain.shape, gain.dtype), pltpu.VMEM(weights.shape, weights.dtype)],
        in_specs=[VMEM] + [HBM] * 5,
        out_specs=[VMEM] * (len(offsets) + 3),
        scratch_shapes=[
            pltpu.VMEM(ids.shape, jnp.int32),
            pltpu.VMEM(gates.shape, F32),
            pltpu.VMEM(partner.shape, jnp.int32),
            pltpu.SemaphoreType.DMA((4,)),
            pltpu.SemaphoreType.DMA((parts,)),
        ],
        compiler_params=pltpu.CompilerParams(vmem_limit_bytes=8 << 20),
        cost_estimate=pl.CostEstimate(
            flops=0, bytes_accessed=2 * weights.size, transcendentals=0
        ),
    )(hidden, *in_hbm(ids, gates, partner, gain, weights))


def hidden_units(rows, gain, weights):
    stacked = jnp.concatenate([r[...].astype(F32) for r in rows], axis=0)
    factor = lax.rsqrt(jnp.mean(stacked * stacked, axis=-1, keepdims=True) + epsilon)
    normed = (stacked * factor * gain[...].astype(F32)).astype(BF16)
    projected = jnp.dot(normed, weights[...], preferred_element_type=F32)
    half = projected.shape[1] // 2
    gate, up = projected[:, :half], projected[:, half:]
    return (gate / (1.0 + jnp.exp(-gate)) * up).astype(BF16)


def early_kernel(count, step, *refs):
    rows, (gain, gate_up, down_at) = refs[:count], refs[count : count + 3]
    outs, (down, down_sem) = refs[count + 3 : 2 * count + 3], refs[2 * count + 3 :]
    copy = pltpu.make_async_copy(down_at, down, down_sem)
    copy.start()
    active = hidden_units(rows, gain, gate_up)
    copy.wait()
    for i in range(down.shape[1] // step):
        at = pl.ds(i * step, step)
        part = jnp.dot(active, down[:, at], preferred_element_type=F32)
        for k in range(count):
            outs[k][:, at] = part[k * CAP : (k + 1) * CAP].astype(BF16)


def early_experts(rows, gain, gate_up, down):
    count = len(rows)
    width = down.shape[1]
    total = count * CAP
    *results, down = pl.pallas_call(
        functools.partial(early_kernel, count, chunk_of(width, 512)),
        out_shape=[jax.ShapeDtypeStruct((CAP, width), BF16)] * count
        + [pltpu.VMEM(down.shape, down.dtype)],
        in_specs=[VMEM] * (count + 2) + [HBM],
        out_specs=[VMEM] * (count + 1),
        scratch_shapes=[pltpu.SemaphoreType.DMA],
        compiler_params=pltpu.CompilerParams(vmem_limit_bytes=(6 << 20) + total * width * 8),
        cost_estimate=pl.CostEstimate(
            flops=2 * total * (gate_up.size + down.size),
            bytes_accessed=2 * (gate_up.size + down.size),
            transcendentals=total * down.shape[0],
        ),
    )(*rows, gain, gate_up, *in_hbm(down))
    return results, down


def late_kernel(count, step, *refs):
    rows, (gain, gate_up, down), outs = refs[:count], refs[count : count + 3], refs[count + 3 :]
    active = hidden_units(rows, gain, gate_up)
    for i in range(down.shape[1] // step):
        at = pl.ds(i * step, step)
        part = jnp.dot(active, down[:, at], preferred_element_type=F32)
        for k in range(count):
            outs[k][:, at] = part[k * CAP : (k + 1) * CAP].astype(BF16)


def late_experts(rows, gain, gate_up, down):
    count = len(rows)
    width = down.shape[1]
    total = count * CAP
    return pl.pallas_call(
        functools.partial(late_kernel, count, chunk_of(width, 512)),
        out_shape=[jax.ShapeDtypeStruct((CAP, width), BF16)] * count,
        in_specs=[VMEM] * (count + 3),
        out_specs=[VMEM] * count,
        compiler_params=pltpu.CompilerParams(vmem_limit_bytes=(6 << 20) + total * width * 8),
        cost_estimate=pl.CostEstimate(
            flops=2 * AHEAD * total * (gate_up.size + down.size),
            bytes_accessed=2 * AHEAD * (gate_up.size + down.size),
            transcendentals=total * down.shape[0],
        ),
    )(*rows, gain, gate_up, down)


def mixing(packed, width, at, used):
    span = (packed.shape[1] - width) // 2
    high = packed[:, width : width + span].astype(F32)[:, at : at + used]
    low = packed[:, width + span :].astype(F32)[:, at : at + used]
    return jnp.concatenate([high, low], axis=0).astype(BF16)


def mixed(matrix, stacked):
    both = jnp.dot(matrix, stacked.astype(BF16), preferred_element_type=F32)
    rows = both.shape[0] // 2
    return both[:rows] + both[rows:]


def begin_kernel(count, step, packed, *refs):
    slots, total = refs[:count], refs[count]
    rows, width = total.shape
    matrix = mixing(packed, width, 0, rows + count * CAP)
    for i in range(width // step):
        at = pl.ds(i * step, step)
        stacked = jnp.concatenate(
            [packed[:, at].astype(F32)] + [s[:, at].astype(F32) for s in slots], axis=0
        )
        total[:, at] = mixed(matrix, stacked)


def begin_combine(packed, slots):
    count = len(slots)
    rows, width = packed.shape[0], slots[0].shape[1]
    return pl.pallas_call(
        functools.partial(begin_kernel, count, chunk_of(width, 512)),
        out_shape=jax.ShapeDtypeStruct((rows, width), F32),
        in_specs=[VMEM] * (count + 1),
        out_specs=VMEM,
        compiler_params=pltpu.CompilerParams(vmem_limit_bytes=8 << 20),
    )(packed, *slots)


def finish_kernel(count, step, begin, packed, total, *refs):
    slots, out_at, out, sems = refs[:count], *refs[count:]
    rows, width = out.shape
    matrix = mixing(packed, width, begin, count * CAP)

    def copy(i):
        at = pl.ds(i * step, step)
        return pltpu.make_async_copy(out.at[:, at], out_at.at[:, at], sems.at[i])

    for i in range(width // step):
        at = pl.ds(i * step, step)
        stacked = jnp.concatenate([s[:, at].astype(F32) for s in slots], axis=0)
        out[:, at] = (total[:, at] + mixed(matrix, stacked)).astype(BF16)
        copy(i).start()
    for i in range(width // step):
        copy(i).wait()


def finish_combine(packed, total, slots, begin):
    count = len(slots)
    rows, width = total.shape
    step = chunk_of(width, 1792)
    return pl.pallas_call(
        functools.partial(finish_kernel, count, step, begin),
        out_shape=jax.ShapeDtypeStruct((rows, width), BF16),
        in_specs=[VMEM] * (count + 2),
        out_specs=HBM,
        scratch_shapes=[
            pltpu.VMEM((rows, width), BF16),
            pltpu.SemaphoreType.DMA((width // step,)),
        ],
        compiler_params=pltpu.CompilerParams(vmem_limit_bytes=8 << 20),
    )(packed, total, *slots)


def shards(hidden, norm_gain, expert_ids, gate_weights, expert_gate_up, expert_down, partner):
    devices = lax.axis_size("ep")
    sections = lax.axis_size("pp")
    section_rows = hidden[0]
    gate_up = expert_gate_up[0, 0]
    down = expert_down[0, 0]

    far, split = devices // 2, max(1, devices * 3 // 4)
    early = [far] + [k for k in range(1, split) if k != far]
    late = list(range(split, devices))
    ids, gates = expert_ids[0].T, gate_weights[0].T
    *picked, rows = route_first(section_rows, ids, devices, early)
    *rest, packed, gain, gate_up = route_rest(
        rows,
        ids,
        gates,
        partner,
        norm_gain,
        gate_up,
        devices,
        late + [0],
        early[::-1] + late + [0],
    )
    picked = dict(zip(early + late + [0], picked + rest))

    def onward(value):
        return lax.ppermute(value, "pp", [(i, (i + 1) % sections) for i in range(sections)])

    def dispatch(value, offset):
        if offset == 0:
            return value
        return lax.ppermute(
            value, "ep", [(i, offset_target(i, offset, devices)) for i in range(devices)]
        )

    def send_back(value, offset):
        return lax.ppermute(
            value,
            ("ep", "pp"),
            [
                (offset_target(i, offset, devices) * sections + p, i * sections + (p + 1) % sections)
                for i in range(devices)
                for p in range(sections)
            ],
        )

    arrived = {k: dispatch(picked[k], k) for k in early + late + [0]}
    packed = onward(packed)
    results, down = early_experts([arrived[k] for k in early + [0]], gain, gate_up, down)
    results = dict(zip(early + [0], results))
    returned = {k: send_back(results[k], k) for k in early[::-1]}
    packed, *held = lax.optimization_barrier((packed, *[arrived[k] for k in late]))
    results.update(zip(late, late_experts(held, gain, gate_up, down)))
    last = late + [0]
    for k, result in zip(last, lax.optimization_barrier([results[k] for k in last])):
        returned[k] = send_back(result, k)
    total = begin_combine(packed, [returned[k] for k in early[::-1]])
    begin = section_rows.shape[0] + len(early) * CAP
    out = finish_combine(packed, total, [returned[k] for k in late + [0]], begin)
    return out[None]


def solution(mesh):
    return jax.shard_map(
        shards,
        mesh=mesh,
        in_specs=(
            P("pp", ("grp", "ep"), None),
            P("pp", None),
            P("pp", ("grp", "ep"), None),
            P("pp", ("grp", "ep"), None),
            P("pp", "ep", None, None),
            P("pp", "ep", None, None),
            P(("grp", "ep"), None),
        ),
        out_specs=P("pp", ("grp", "ep"), None),
        check_vma=False,
    )
```

```python
import functools

import jax
import jax.numpy as jnp
from jax import lax
from jax.experimental import pallas as pl
from jax.experimental.pallas import tpu as pltpu
from jax.sharding import PartitionSpec as P

EXPERTS = 4
TOP = 2
CAP = 24
AHEAD = 8

guidance_scale = 2.5
epsilon = 1e-06
F32 = jnp.float32
BF16 = jnp.bfloat16
VMEM = pl.BlockSpec(memory_space=pltpu.VMEM)
HBM = pl.BlockSpec(memory_space=pltpu.HBM)


def chunk_of(extent, largest):
    size = largest
    while extent % size:
        size //= 2
    return size


def in_hbm(*arrays):
    return [pltpu.with_memory_space_constraint(a, pltpu.HBM) for a in arrays]


def lanes_for(extent):
    return -(-extent // 128) * 128


def offset_target(me, offset, devices):
    if devices & (devices - 1) == 0:
        return me ^ offset
    return (me + offset) % devices


def fetch(pairs, sems, others=()):
    copies = [pltpu.make_async_copy(s, d, sems.at[i]) for i, (s, d) in enumerate(pairs)]
    for copy in [*copies, *others]:
        copy.start()
    for copy in copies:
        copy.wait()


def slot_positions(ids, rows):
    line = lax.broadcasted_iota(jnp.int32, (rows, rows), 0)
    lane = lax.broadcasted_iota(jnp.int32, (rows, rows), 1)
    expert = lax.broadcasted_iota(jnp.int32, (EXPERTS, rows), 0)
    named = jnp.zeros((EXPERTS, rows), F32)
    for k in range(TOP):
        named = named + (ids[k : k + 1, :] == expert).astype(F32)
    position = jnp.dot(
        named.astype(BF16), (line < lane).astype(F32).astype(BF16), preferred_element_type=F32
    )
    return jnp.where(named > 0.0, position, -1.0)


def of_expert(table, own):
    expert = lax.broadcasted_iota(jnp.int32, table.shape, 0)
    return jnp.sum(jnp.where(expert == own, table, 0.0), axis=0, keepdims=True)


def choice_of(position, own, rows):
    slot = lax.broadcasted_iota(jnp.int32, (CAP, rows), 0).astype(F32)
    return (of_expert(position, own) == slot).astype(F32)


def pick(choice, rows):
    return jnp.dot(choice.astype(BF16), rows, preferred_element_type=F32).astype(BF16)


def first_kernel(devices, offsets, hidden_at, ids_at, *refs):
    picked, (hidden, ids, sems) = refs[: len(offsets)], refs[len(offsets) :]
    pairs = [(ids_at, ids), (hidden_at, hidden)]
    copies = [pltpu.make_async_copy(s, d, sems.at[i]) for i, (s, d) in enumerate(pairs)]
    for copy in copies:
        copy.start()
    rows, _ = hidden.shape
    copies[0].wait()
    position = slot_positions(ids, rows)
    me = lax.axis_index("ep")
    owners = [offset_target(me, k, devices) // (devices // EXPERTS) for k in offsets]
    choices = jnp.concatenate([choice_of(position, own, rows) for own in owners], axis=0)
    copies[1].wait()
    taken = jnp.dot(choices.astype(BF16), hidden[...], preferred_element_type=F32)
    for k, ref in enumerate(picked):
        ref[...] = taken[k * CAP : (k + 1) * CAP].astype(BF16)


def route_first(hidden, ids, devices, offsets):
    rows, width = hidden.shape
    return pl.pallas_call(
        functools.partial(first_kernel, devices, offsets),
        out_shape=[jax.ShapeDtypeStruct((CAP, width), BF16)] * len(offsets)
        + [pltpu.VMEM((rows, width), BF16)],
        in_specs=[HBM] * 2,
        out_specs=[VMEM] * (len(offsets) + 1),
        scratch_shapes=[pltpu.VMEM(ids.shape, jnp.int32), pltpu.SemaphoreType.DMA((2,))],
        compiler_params=pltpu.CompilerParams(vmem_limit_bytes=8 << 20),
    )(*in_hbm(hidden, ids))


def rest_kernel(
    devices, offsets, order, parts, hidden, ids_at, gates_at, partner_at, gain_at, weights_at, *refs
):
    picked, (packed, gain, weights) = refs[: len(offsets)], refs[len(offsets) : len(offsets) + 3]
    ids, gates, partner, sems, weight_sems = refs[len(offsets) + 3 :]
    rows, width = hidden.shape
    size = weights.shape[0] // parts
    copies = [
        pltpu.make_async_copy(
            weights_at.at[pl.ds(i * size, size)], weights.at[pl.ds(i * size, size)], weight_sems.at[i]
        )
        for i in range(parts)
    ]
    fetch(
        [
            (ids_at, ids),
            (gates_at, gates),
            (partner_at, partner),
            (gain_at, gain),
        ],
        sems,
        copies,
    )
    middle = rows // 2
    me = lax.axis_index("ep")
    is_last = (lax.axis_index("pp") == lax.axis_size("pp") - 1).astype(jnp.int32)
    position = slot_positions(ids, rows)
    expert = lax.broadcasted_iota(jnp.int32, (EXPERTS, rows), 0)
    weight = jnp.zeros((EXPERTS, rows), F32)
    for k in range(TOP):
        weight = weight + jnp.where(ids[k : k + 1, :] == expert, gates[k : k + 1, :], 0.0)

    line = lax.broadcasted_iota(jnp.int32, (rows, rows), 0)
    lane = lax.broadcasted_iota(jnp.int32, (rows, rows), 1)
    same_row = (line == lane).astype(F32)
    weighted = [same_row]
    for offset in order:
        own = offset_target(me, offset, devices) // (devices // EXPERTS)
        choice = choice_of(position, own, rows)
        weighted.append(choice * of_expert(weight, own))
        if offset in offsets:
            picked[offsets.index(offset)][...] = pick(choice, hidden[...])

    pair_line = lax.broadcasted_iota(jnp.int32, (rows, middle), 0)
    pair_lane = lax.broadcasted_iota(jnp.int32, (rows, middle), 1)
    pair = jnp.sum(
        jnp.where(pair_line == pair_lane, partner[...].astype(F32), 0.0), axis=1, keepdims=True
    )
    weak_row = (lane.astype(F32) == pair + float(middle)).astype(F32)
    guided = guidance_scale * same_row + (1.0 - guidance_scale) * weak_row
    guide = jnp.where(jnp.logical_and(line < middle, is_last > 0), guided, same_row)
    span = (packed.shape[1] - width) // 2
    if span > rows + devices * CAP:
        weighted.append(jnp.zeros((span - rows - devices * CAP, rows), F32))
    mix = lax.dot_general(
        guide,
        jnp.concatenate(weighted, axis=0),
        (((1,), (1,)), ((), ())),
        precision=lax.Precision.HIGHEST,
        preferred_element_type=F32,
    )
    high = mix.astype(BF16)
    packed[:, :width] = hidden[...]
    packed[:, width : width + span] = high
    packed[:, width + span :] = (mix - high.astype(F32)).astype(BF16)
    for copy in copies:
        copy.wait()


def route_rest(hidden, ids, gates, partner, gain, weights, devices, offsets, order):
    parts = 7 if weights.shape[0] % 112 == 0 else 1
    rows, width = hidden.shape
    span = lanes_for(rows + devices * CAP)
    return pl.pallas_call(
        functools.partial(rest_kernel, devices, offsets, order, parts),
        out_shape=[jax.ShapeDtypeStruct((CAP, width), BF16)] * len(offsets)
        + [jax.ShapeDtypeStruct((rows, width + 2 * span), BF16)]
        + [pltpu.VMEM(gain.shape, gain.dtype), pltpu.VMEM(weights.shape, weights.dtype)],
        in_specs=[VMEM] + [HBM] * 5,
        out_specs=[VMEM] * (len(offsets) + 3),
        scratch_shapes=[
            pltpu.VMEM(ids.shape, jnp.int32),
            pltpu.VMEM(gates.shape, F32),
            pltpu.VMEM(partner.shape, jnp.int32),
            pltpu.SemaphoreType.DMA((4,)),
            pltpu.SemaphoreType.DMA((parts,)),
        ],
        compiler_params=pltpu.CompilerParams(vmem_limit_bytes=8 << 20),
        cost_estimate=pl.CostEstimate(
            flops=0, bytes_accessed=2 * weights.size, transcendentals=0
        ),
    )(hidden, *in_hbm(ids, gates, partner, gain, weights))


def hidden_units(rows, gain, weights):
    stacked = jnp.concatenate([r[...].astype(F32) for r in rows], axis=0)
    factor = lax.rsqrt(jnp.mean(stacked * stacked, axis=-1, keepdims=True) + epsilon)
    normed = (stacked * factor * gain[...].astype(F32)).astype(BF16)
    projected = jnp.dot(normed, weights[...], preferred_element_type=F32)
    half = projected.shape[1] // 2
    gate, up = projected[:, :half], projected[:, half:]
    return (gate / (1.0 + jnp.exp(-gate)) * up).astype(BF16)


def early_kernel(count, step, *refs):
    rows, (gain, gate_up, down_at) = refs[:count], refs[count : count + 3]
    outs, (down, down_sem) = refs[count + 3 : 2 * count + 3], refs[2 * count + 3 :]
    copy = pltpu.make_async_copy(down_at, down, down_sem)
    copy.start()
    active = hidden_units(rows, gain, gate_up)
    copy.wait()
    for i in range(down.shape[1] // step):
        at = pl.ds(i * step, step)
        part = jnp.dot(active, down[:, at], preferred_element_type=F32)
        for k in range(count):
            outs[k][:, at] = part[k * CAP : (k + 1) * CAP].astype(BF16)


def early_experts(rows, gain, gate_up, down):
    count = len(rows)
    width = down.shape[1]
    total = count * CAP
    *results, down = pl.pallas_call(
        functools.partial(early_kernel, count, chunk_of(width, 512)),
        out_shape=[jax.ShapeDtypeStruct((CAP, width), BF16)] * count
        + [pltpu.VMEM(down.shape, down.dtype)],
        in_specs=[VMEM] * (count + 2) + [HBM],
        out_specs=[VMEM] * (count + 1),
        scratch_shapes=[pltpu.SemaphoreType.DMA],
        compiler_params=pltpu.CompilerParams(vmem_limit_bytes=(6 << 20) + total * width * 8),
        cost_estimate=pl.CostEstimate(
            flops=2 * total * (gate_up.size + down.size),
            bytes_accessed=2 * (gate_up.size + down.size),
            transcendentals=total * down.shape[0],
        ),
    )(*rows, gain, gate_up, *in_hbm(down))
    return results, down


def late_kernel(count, step, *refs):
    rows, (gain, gate_up, down), outs = refs[:count], refs[count : count + 3], refs[count + 3 :]
    active = hidden_units(rows, gain, gate_up)
    for i in range(down.shape[1] // step):
        at = pl.ds(i * step, step)
        part = jnp.dot(active, down[:, at], preferred_element_type=F32)
        for k in range(count):
            outs[k][:, at] = part[k * CAP : (k + 1) * CAP].astype(BF16)


def late_experts(rows, gain, gate_up, down):
    count = len(rows)
    width = down.shape[1]
    total = count * CAP
    return pl.pallas_call(
        functools.partial(late_kernel, count, chunk_of(width, 512)),
        out_shape=[jax.ShapeDtypeStruct((CAP, width), BF16)] * count,
        in_specs=[VMEM] * (count + 3),
        out_specs=[VMEM] * count,
        compiler_params=pltpu.CompilerParams(vmem_limit_bytes=(6 << 20) + total * width * 8),
        cost_estimate=pl.CostEstimate(
            flops=2 * AHEAD * total * (gate_up.size + down.size),
            bytes_accessed=2 * AHEAD * (gate_up.size + down.size),
            transcendentals=total * down.shape[0],
        ),
    )(*rows, gain, gate_up, down)


def mixing(packed, width, at, used):
    span = (packed.shape[1] - width) // 2
    high = packed[:, width : width + span].astype(F32)[:, at : at + used]
    low = packed[:, width + span :].astype(F32)[:, at : at + used]
    return jnp.concatenate([high, low], axis=0).astype(BF16)


def mixed(matrix, stacked):
    both = jnp.dot(matrix, stacked.astype(BF16), preferred_element_type=F32)
    rows = both.shape[0] // 2
    return both[:rows] + both[rows:]


def begin_kernel(count, step, packed, *refs):
    slots, total = refs[:count], refs[count]
    rows, width = total.shape
    matrix = mixing(packed, width, 0, rows + count * CAP)
    for i in range(width // step):
        at = pl.ds(i * step, step)
        stacked = jnp.concatenate(
            [packed[:, at].astype(F32)] + [s[:, at].astype(F32) for s in slots], axis=0
        )
        total[:, at] = mixed(matrix, stacked)


def begin_combine(packed, slots):
    count = len(slots)
    rows, width = packed.shape[0], slots[0].shape[1]
    return pl.pallas_call(
        functools.partial(begin_kernel, count, chunk_of(width, 512)),
        out_shape=jax.ShapeDtypeStruct((rows, width), F32),
        in_specs=[VMEM] * (count + 1),
        out_specs=VMEM,
        compiler_params=pltpu.CompilerParams(vmem_limit_bytes=8 << 20),
    )(packed, *slots)


def finish_kernel(count, step, begin, packed, total, *refs):
    slots, out_at, out, sems = refs[:count], *refs[count:]
    rows, width = out.shape
    matrix = mixing(packed, width, begin, count * CAP)

    def copy(i):
        at = pl.ds(i * step, step)
        return pltpu.make_async_copy(out.at[:, at], out_at.at[:, at], sems.at[i])

    for i in range(width // step):
        at = pl.ds(i * step, step)
        stacked = jnp.concatenate([s[:, at].astype(F32) for s in slots], axis=0)
        out[:, at] = (total[:, at] + mixed(matrix, stacked)).astype(BF16)
        copy(i).start()
    for i in range(width // step):
        copy(i).wait()


def finish_combine(packed, total, slots, begin):
    count = len(slots)
    rows, width = total.shape
    step = chunk_of(width, 512)
    return pl.pallas_call(
        functools.partial(finish_kernel, count, step, begin),
        out_shape=jax.ShapeDtypeStruct((rows, width), BF16),
        in_specs=[VMEM] * (count + 2),
        out_specs=HBM,
        scratch_shapes=[
            pltpu.VMEM((rows, width), BF16),
            pltpu.SemaphoreType.DMA((width // step,)),
        ],
        compiler_params=pltpu.CompilerParams(vmem_limit_bytes=8 << 20),
    )(packed, total, *slots)


def shards(hidden, norm_gain, expert_ids, gate_weights, expert_gate_up, expert_down, partner):
    devices = lax.axis_size("ep")
    sections = lax.axis_size("pp")
    section_rows = hidden[0]
    gate_up = expert_gate_up[0, 0]
    down = expert_down[0, 0]

    far, split = devices // 2, max(1, devices * 3 // 4)
    early = [far] + [k for k in range(1, split) if k != far]
    late = list(range(split, devices))
    ids, gates = expert_ids[0].T, gate_weights[0].T
    *picked, rows = route_first(section_rows, ids, devices, early)
    *rest, packed, gain, gate_up = route_rest(
        rows,
        ids,
        gates,
        partner,
        norm_gain,
        gate_up,
        devices,
        late + [0],
        early[::-1] + late + [0],
    )
    picked = dict(zip(early + late + [0], picked + rest))

    def onward(value):
        return lax.ppermute(value, "pp", [(i, (i + 1) % sections) for i in range(sections)])

    def dispatch(value, offset):
        if offset == 0:
            return value
        return lax.ppermute(
            value, "ep", [(i, offset_target(i, offset, devices)) for i in range(devices)]
        )

    def send_back(value, offset):
        return lax.ppermute(
            value,
            ("ep", "pp"),
            [
                (offset_target(i, offset, devices) * sections + p, i * sections + (p + 1) % sections)
                for i in range(devices)
                for p in range(sections)
            ],
        )

    arrived = {k: dispatch(picked[k], k) for k in early + late + [0]}
    packed = onward(packed)
    results, down = early_experts([arrived[k] for k in early], gain, gate_up, down)
    results = dict(zip(early, results))
    returned = {k: send_back(results[k], k) for k in early[::-1]}
    packed, *held = lax.optimization_barrier((packed, *[arrived[k] for k in late + [0]]))
    results.update(zip(late + [0], late_experts(held, gain, gate_up, down)))
    last = late + [0]
    for k, result in zip(last, lax.optimization_barrier([results[k] for k in last])):
        returned[k] = send_back(result, k)
    total = begin_combine(packed, [returned[k] for k in early[::-1]])
    begin = section_rows.shape[0] + len(early) * CAP
    out = finish_combine(packed, total, [returned[k] for k in late + [0]], begin)
    return out[None]


def solution(mesh):
    return jax.shard_map(
        shards,
        mesh=mesh,
        in_specs=(
            P("pp", ("grp", "ep"), None),
            P("pp", None),
            P("pp", ("grp", "ep"), None),
            P("pp", ("grp", "ep"), None),
            P("pp", "ep", None, None),
            P("pp", "ep", None, None),
            P(("grp", "ep"), None),
        ),
        out_specs=P("pp", ("grp", "ep"), None),
        check_vma=False,
    )
```
